32 devices in a mesh: section: 2 (over y), dp: 16 (over z, x, core).
Axes of the slice: x: 2, y: 2, z: 4, core: 2. Of those that a mesh axis runs over, the one named last changes fastest.
Arguments:
- layer_input: bfloat16 [2, 4096, 4, 128], P('section', 'dp'), may hold values from 0 to 1
- gate_weight: bfloat16 [2, 4096, 16384], P('section', None, 'dp'), may hold values from -0.09375 to 0.09375
- up_weight: bfloat16 [2, 4096, 16384], P('section', None, 'dp'), may hold values from -0.09375 to 0.09375
- down_weight: bfloat16 [2, 16384, 4096], P('section', 'dp'), may hold values from -0.046875 to 0.046875
- hidden_threshold: int32 [2, 16384], P('section', 'dp'), may hold values from 1 to 5
- hidden_width: int32 [2, 16384], P('section', 'dp'), may hold values from 1 to 5
- out_threshold: int32 [2, 4096], P('section', 'dp'), may hold values from 1 to 5
- out_width: int32 [2, 4096], P('section', 'dp'), may hold values from 1 to 5
- out_cotangent: bfloat16 [2, 4096, 4, 128], P('section', 'dp'), may hold values from -6 to 6
Outputs:
- incoming_spikes: bfloat16 [2, 4096, 4, 128], P('section', 'dp')
- returned_grads: bfloat16 [2, 4096, 4, 128], P('section', 'dp')
The draws below stay inside these ranges and needn't reach their ends.
All inputs are finite; a program needn't handle non-finite values.
Results may differ from the reference program's by a relative error of at most 0.013.
Values may be sent and summed in bfloat16 or wider, within the bound.
No kernel may reach another device: no remote copies, remote signals or barrier semaphores. Data moves between devices by JAX's collectives and lax.ppermute only.
A program may use at most 128 MiB of HBM per device.

```python
import jax
import jax.numpy as jnp
from jax import lax

D = 4096
FFW = 16384
T_STEPS = 4
TOK = 128
SECTIONS = 2


def with_ends(array, key, smallest, largest):
    shape = array.shape
    index_at = [jax.random.randint(jax.random.fold_in(key, axis), (), 0, shape[axis]) for axis in range(len(shape))]
    array = array.at[tuple(index_at)].set(smallest)
    longest = shape.index(max(shape))
    index_at[longest] = (index_at[longest] + 1) % shape[longest]
    return array.at[tuple(index_at)].set(largest)


def steps_of(own_key, shape, split, least, top_value):
    def one(axis_at, blocks):
        steps = jax.random.uniform(jax.random.fold_in(jax.random.fold_in(own_key, 6), axis_at), (blocks,), jnp.float32, least / len(split), top_value / len(split))
        return jnp.repeat(jnp.exp(steps), shape[axis_at] // blocks).reshape((-1,) + (1,) * (len(shape) - axis_at - 1))

    factor_of = one(*split[0])
    for cut in split[1:]:
        factor_of = factor_of * one(*cut)
    return factor_of


def normal_values(key, shape, deviation, most, pieces=(), held_as=jnp.bfloat16):
    values = jax.random.normal(key, shape, jnp.float32) * deviation
    if len(pieces) > 0:
        values = steps_of(key, shape, pieces, -0.22, 0.18) * values
    return jnp.clip(values, min=-most, max=most).astype(held_as)


def setup_inputs(seed: int = 0) -> dict:
    keys = jax.random.split(jax.random.key(seed), 10)
    layer_input = jnp.clip(1.0 * jax.random.uniform(keys[0], (SECTIONS, D, T_STEPS, TOK), jnp.float32) ** steps_of(keys[0], (SECTIONS, D, T_STEPS, TOK), ((0, 2), (1, 16)), -0.2, 0.2), 0.0, 1.0).astype(jnp.bfloat16)
    gate_weight = normal_values(keys[1], (SECTIONS, D, FFW), D ** -0.5, 0.09375, ((0, 2), (2, 16)))
    up_weight = normal_values(keys[2], (SECTIONS, D, FFW), D ** -0.5, 0.09375, ((0, 2), (2, 16)))
    down_weight = normal_values(keys[3], (SECTIONS, FFW, D), FFW ** -0.5, 0.046875, ((0, 2), (1, 16)))
    hidden_threshold = with_ends(jax.random.randint(keys[4], (SECTIONS, FFW), 1, 6), jax.random.fold_in(keys[4], 1), 1, 5).astype(jnp.int32)
    hidden_width = with_ends(jax.random.randint(keys[5], (SECTIONS, FFW), 1, 6), jax.random.fold_in(keys[5], 1), 1, 5).astype(jnp.int32)
    out_threshold = with_ends(jax.random.randint(keys[6], (SECTIONS, D), 1, 6), jax.random.fold_in(keys[6], 1), 1, 5).astype(jnp.int32)
    out_width = with_ends(jax.random.randint(keys[7], (SECTIONS, D), 1, 6), jax.random.fold_in(keys[7], 1), 1, 5).astype(jnp.int32)
    out_cotangent = normal_values(keys[8], (SECTIONS, D, T_STEPS, TOK), 1.0, 6.0, ((0, 2), (1, 16)))
    return {"layer_input": layer_input, "gate_weight": gate_weight, "up_weight": up_weight, "down_weight": down_weight, "hidden_threshold": hidden_threshold, "hidden_width": hidden_width, "out_threshold": out_threshold, "out_width": out_width, "out_cotangent": out_cotangent}


decay_rate = 0.9
level_unit = 0.125

def soft_spikes(currents, threshold_level, width_level):
    threshold = level_unit * threshold_level.astype(currents[0].dtype)
    width = level_unit * width_level.astype(currents[0].dtype)
    potential = jnp.zeros_like(currents[0])
    spikes = jnp.zeros_like(currents[0])
    emitted = []
    for current in currents:
        potential = decay_rate * (potential - threshold * spikes) + current
        spikes = jax.nn.sigmoid((potential - threshold) / width)
        emitted.append(spikes)
    return emitted

def split_steps(matrix, count, axis):
    return [lax.slice_in_dim(matrix, k * count, (k + 1) * count, axis=axis) for k in range(T_STEPS)]

def run_section(inputs, gate_w, up_w, down_w, hid_level, hid_spread, out_level, out_spread, out_grad):
    rows = T_STEPS * TOK
    inputs_flat = inputs.reshape(D, rows)
    gate = jnp.dot(inputs_flat.T, gate_w, preferred_element_type=jnp.float32)
    upward = jnp.dot(inputs_flat.T, up_w, preferred_element_type=jnp.float32)

    def hidden_fn(gate_in, up_in):
        return soft_spikes(split_steps(jax.nn.silu(gate_in) * up_in, TOK, 0), hid_level, hid_spread)
    hidden_list, hidden_back = jax.vjp(hidden_fn, gate, upward)
    spikes = jnp.concatenate(hidden_list, 0).astype(jnp.bfloat16)
    current = jnp.dot(spikes, down_w, preferred_element_type=jnp.float32) + inputs_flat.T.astype(jnp.float32)

    def out_fn(total):
        return soft_spikes(split_steps(total, TOK, 0), out_level, out_spread)
    out_list, out_back = jax.vjp(out_fn, current)
    emitted = jnp.concatenate(out_list, 0).astype(jnp.bfloat16)
    cotangent = out_grad.reshape(D, rows).T.astype(jnp.float32)
    current_grad = out_back(split_steps(cotangent, TOK, 0))[0]
    spike_grad = jnp.dot(current_grad.astype(jnp.bfloat16), down_w.T, preferred_element_type=jnp.float32)
    gate_grad, up_grad = hidden_back(split_steps(spike_grad, TOK, 0))
    input_grad = jnp.dot(gate_grad.astype(jnp.bfloat16), gate_w.T, preferred_element_type=jnp.float32)
    input_grad = input_grad + jnp.dot(up_grad.astype(jnp.bfloat16), up_w.T, preferred_element_type=jnp.float32)
    input_grad = (input_grad + current_grad).astype(jnp.bfloat16)
    return (emitted.T.reshape(D, T_STEPS, TOK), input_grad.T.reshape(D, T_STEPS, TOK))

def reference(layer_input, gate_weight, up_weight, down_weight, hidden_threshold, hidden_width, out_threshold, out_width, out_cotangent):
    emitted_all = []
    grads_all = []
    for section in range(SECTIONS):
        emitted, input_grad = run_section(layer_input[section], gate_weight[section], up_weight[section], down_weight[section], hidden_threshold[section], hidden_width[section], out_threshold[section], out_width[section], out_cotangent[section])
        emitted_all.append(emitted)
        grads_all.append(input_grad)
    zeros = jnp.zeros((1, D, T_STEPS, TOK), jnp.bfloat16)
    incoming = jnp.concatenate([zeros] + [e[None] for e in emitted_all[:-1]], 0)
    returned = jnp.concatenate([g[None] for g in grads_all[1:]] + [zeros], 0)
    return (incoming, returned)
```

```python
import functools

import jax
import jax.numpy as jnp
from jax import lax
from jax.experimental import pallas as pl
from jax.experimental.pallas import tpu as pltpu
from jax.sharding import PartitionSpec as P

decay_rate = 0.9
level_unit = 0.125
f32 = jnp.float32
bf16 = jnp.bfloat16
VMEM_LIMIT = 16 * 1024 * 1024


def in_vmem(x):
    return pltpu.with_memory_space_constraint(x, pltpu.VMEM)


def call(kernel, outs, *args, places=None, aliases=None):
    specs = []
    given = []
    for a in args:
        if a.dtype == jnp.int32 and a.ndim == 1:
            specs.append(pl.BlockSpec(memory_space=pltpu.SMEM))
            given.append(a)
        else:
            specs.append(pl.BlockSpec(memory_space=pltpu.VMEM))
            given.append(in_vmem(a))
    return pl.pallas_call(
        kernel,
        out_shape=[pltpu.VMEM(shape, dtype) for shape, dtype in outs],
        in_specs=specs,
        out_specs=[pl.BlockSpec(memory_space=pltpu.VMEM)] * len(outs),
        input_output_aliases=aliases or {},
        compiler_params=pltpu.CompilerParams(vmem_limit_bytes=VMEM_LIMIT),
    )(*given)


def nn(left, right):
    return lax.dot_general(left, right, (((1,), (0,)), ((), ())), preferred_element_type=f32)


def nt(left, right):
    return lax.dot_general(left, right, (((1,), (1,)), ((), ())), preferred_element_type=f32)


def tiles(total, width):
    width = min(width, total)
    return [slice(k, k + width) for k in range(0, total, width)]


def levels(threshold_ref, width_ref, at):
    threshold = level_unit * threshold_ref[:, at].astype(f32)
    scale = 1.0 / (level_unit * width_ref[:, at].astype(f32))
    return threshold, scale


def spikes_of(currents, threshold, scale):
    potential = None
    out = []
    for current in currents:
        if potential is None:
            potential = current
        else:
            potential = decay_rate * (potential - threshold * out[-1]) + current
        out.append(jax.nn.sigmoid((potential - threshold) * scale))
    return out


def spikes_back(spikes, cotangents, threshold, scale):
    after = None
    grads = [None] * len(spikes)
    for t in reversed(range(len(spikes))):
        slope = spikes[t] * (1.0 - spikes[t]) * scale
        if after is None:
            after = cotangents[t] * slope
        else:
            after = (cotangents[t] - decay_rate * threshold * after) * slope + decay_rate * after
        grads[t] = after
    return grads


def step_rows(count, tokens):
    return [slice(t * tokens, (t + 1) * tokens) for t in range(count)]


def whole_pieces(refs, shape):
    out = []
    pending = None
    for ref in refs:
        if ref.shape == shape:
            out.append(ref[...])
        elif pending is None:
            pending = ref[...]
        else:
            out.append(jnp.concatenate([pending, ref[...]], axis=0))
            pending = None
    return out


def gate_up_kernel(n_pieces, first, last, steps, tokens, *refs):
    at, refs = refs[0], list(refs[1:])
    piece_refs, refs = refs[:n_pieces], refs[n_pieces:]
    gate_w, up_w = refs[:2]
    refs = refs[2:]
    if not first:
        acc = refs[:2]
        refs = refs[2:]
    if last:
        threshold_ref, width_ref = refs[:2]
        refs = refs[2:]
    gate_out, up_out = refs[:2]
    rows = steps * tokens
    local = next(r.shape[1] for r in piece_refs)
    pieces = whole_pieces(piece_refs, (rows, local))
    left = jnp.concatenate(pieces, axis=1)
    for cols in tiles(gate_out.shape[1], 256):
        both = []
        for which, weight in enumerate((gate_w, up_w)):
            right = jnp.concatenate(
                [weight[pl.ds(pl.multiple_of(at[p], local), local), cols] for p in range(len(pieces))],
                axis=0,
            )
            total = nn(left, right)
            if not first:
                total = total + acc[which][:, cols]
            both.append(total)
            (gate_out, up_out)[which][:, cols] = total
        if last:
            threshold, scale = levels(threshold_ref, width_ref, cols)
            hidden = both[0] * jax.nn.sigmoid(both[0]) * both[1]
            parts = [hidden[r] for r in step_rows(steps, tokens)]
            out = spikes_of(parts, threshold, scale)
            refs[2][:, cols] = jnp.concatenate(out, axis=0).astype(bf16)


def down_kernel(n_own, n_blocks, at, spikes, down, *outs):
    left = spikes[...]
    for p in range(n_blocks):
        out = outs[p]
        local = out.shape[1]
        right = down[:, pl.ds(pl.multiple_of(at[p], local), local)]
        out[...] = nn(left, right).astype(out.dtype)


def out_kernel(steps, tokens, own, sib, fw, bw, x, cot, threshold_ref, width_ref, emitted, grad, grad16):
    threshold, scale = levels(threshold_ref, width_ref, slice(None))
    current = (
        own[...] + sib[...].astype(f32) + fw[...].astype(f32) + bw[...].astype(f32) + x[...].astype(f32)
    )
    rows = step_rows(steps, tokens)
    out = spikes_of([current[r] for r in rows], threshold, scale)
    emitted[...] = jnp.concatenate(out, axis=0).astype(bf16)
    grads = spikes_back(out, [cot[r, :].astype(f32) for r in rows], threshold, scale)
    total = jnp.concatenate(grads, axis=0)
    grad[...] = total
    grad16[...] = total.astype(bf16)


def spike_grad_kernel(n_pieces, first, last, steps, tokens, *refs):
    at, refs = refs[0], list(refs[1:])
    piece_refs, refs = refs[:n_pieces], refs[n_pieces:]
    down = refs[0]
    refs = refs[1:]
    if not first:
        acc = refs[0]
        refs = refs[1:]
    if last:
        gate, up, threshold_ref, width_ref = refs[:4]
        refs = refs[4:]
    rows = steps * tokens
    local = next(r.shape[1] for r in piece_refs)
    pieces = whole_pieces(piece_refs, (rows, local))
    left = jnp.concatenate(pieces, axis=1)
    for hid in tiles(down.shape[0], 256):
        right = jnp.concatenate(
            [down[hid, pl.ds(pl.multiple_of(at[p], local), local)] for p in range(len(pieces))], axis=1
        )
        total = nt(left, right)
        if not first:
            total = total + acc[:, hid]
        if not last:
            refs[0][:, hid] = total
            continue
        threshold, scale = levels(threshold_ref, width_ref, hid)
        gate_in, up_in = gate[:, hid], up[:, hid]
        sig = jax.nn.sigmoid(gate_in)
        act = gate_in * sig
        hidden = act * up_in
        parts = step_rows(steps, tokens)
        out = spikes_of([hidden[r] for r in parts], threshold, scale)
        grads = spikes_back(out, [total[r] for r in parts], threshold, scale)
        grad = jnp.concatenate(grads, axis=0)
        refs[0][:, hid] = (grad * up_in * (sig * (1.0 + gate_in * (1.0 - sig)))).astype(bf16)
        refs[1][:, hid] = (grad * act).astype(bf16)


def input_grad_kernel(n_blocks, at, gate_grad, up_grad, gate_w, up_w, *outs):
    left = jnp.concatenate([gate_grad[...], up_grad[...]], axis=1)
    for p in range(n_blocks):
        out = outs[p]
        local = out.shape[1]
        here = pl.ds(pl.multiple_of(at[p], local), local)
        right = jnp.concatenate([gate_w[here, :], up_w[here, :]], axis=1)
        out[...] = nt(left, right).astype(out.dtype)


def per_device(
    devices,
    layer_input,
    gate_weight,
    up_weight,
    down_weight,
    hidden_threshold,
    hidden_width,
    out_threshold,
    out_width,
    out_cotangent,
):
    local = layer_input.shape[1]
    steps = layer_input.shape[2]
    tokens = layer_input.shape[3]
    rows = steps * tokens
    half = rows // 2
    hid = gate_weight.shape[2]
    chips = devices // 2
    far = chips // 2
    side = chips // 2

    def chip_at(place):
        place = place % chips
        return jnp.where(place < side, 2 * place, 2 * (chips - 1 - place) + 1)

    order = [2 * p if p < side else 2 * (chips - 1 - p) + 1 for p in range(chips)]
    forward, backward, sibling = [], [], []
    for p in range(chips):
        a, b = order[p], order[(p + 1) % chips]
        for core in range(2):
            forward.append((2 * a + core, 2 * b + core))
            backward.append((2 * b + core, 2 * a + core))
            sibling.append((2 * a + core, 2 * a + 1 - core))
    send_fw = lambda v: lax.ppermute(v, "dp", forward)
    send_bw = lambda v: lax.ppermute(v, "dp", backward)
    swap = lambda v: lax.ppermute(v, "dp", sibling)

    index = lax.axis_index("dp").astype(jnp.int32)
    chip, core = index // 2, index % 2
    place = jnp.where(chip % 2 == 0, chip // 2, chips - 1 - chip // 2)

    def block_at(distance, sib):
        which = 2 * chip_at(place + distance) + (1 - core if sib else core)
        return which * local

    gate_w, up_w, down_w = gate_weight[0], up_weight[0], down_weight[0]
    x = jnp.transpose(layer_input[0], (1, 2, 0)).reshape(rows, local)
    cot = jnp.transpose(out_cotangent[0], (1, 2, 0)).reshape(rows, local)

    def gathered(mine):
        groups = [([mine, swap(mine)], [(0, False), (0, True)])]
        fw = bw = mine
        for k in range(1, far + 1):
            if k == far:
                fw, bw = fw[:half], bw[half:]
            fw, bw = send_fw(fw), send_bw(bw)
            if k < far:
                groups.append(
                    (
                        [fw, bw, swap(fw), swap(bw)],
                        [(-k, False), (k, False), (-k, True), (k, True)],
                    )
                )
            else:
                groups.append(([fw, bw, swap(fw), swap(bw)], [(-k, False), (-k, True)]))
        return groups

    def places(at):
        return jnp.stack([block_at(d, s) for d, s in at]).astype(jnp.int32)

    def scattered(blocks_of):
        own, sib = blocks_of([far])
        sib = [swap(s) for s in sib]
        total = own[0] + sib[0].astype(f32)
        fw, bw = total[:half].astype(bf16), total[half:].astype(bf16)
        for k in range(far - 1, 0, -1):
            fw, bw = send_fw(fw), send_bw(bw)
            own, sib = blocks_of([k, -k])
            sib = [swap(s) for s in sib]
            a, b = own[0] + sib[0].astype(f32), own[1] + sib[1].astype(f32)
            if k == far - 1:
                fw = jnp.concatenate([a[:half] + fw.astype(f32), a[half:]], axis=0).astype(bf16)
                bw = jnp.concatenate([b[:half], b[half:] + bw.astype(f32)], axis=0).astype(bf16)
            else:
                fw, bw = (a + fw.astype(f32)).astype(bf16), (b + bw.astype(f32)).astype(bf16)
        fw, bw = send_fw(fw), send_bw(bw)
        own, sib = blocks_of([0])
        return own[0], swap(sib[0]), fw, bw

    acc = None
    groups = gathered(x)
    hid_level, hid_spread = hidden_threshold, hidden_width
    for k, (pieces, at) in enumerate(groups):
        first, last = k == 0, k == len(groups) - 1
        args = [places(at), *pieces, gate_w, up_w]
        aliases = {}
        if not first:
            aliases = {len(args): 0, len(args) + 1: 1}
            args += list(acc)
        outs = [((rows, hid), f32)] * 2
        if last:
            args += [hid_level, hid_spread]
            outs = outs + [((rows, hid), bf16)]
        res = call(
            functools.partial(gate_up_kernel, len(pieces), first, last, steps, tokens),
            outs,
            *args,
            aliases=aliases,
        )
        acc = res[:2]
    gate, upward, spikes = res

    def down_blocks(distances):
        at = [(d, s) for s in (False, True) for d in distances]
        outs = [((rows, local), bf16 if s else f32) for _, s in at]
        res = call(
            functools.partial(down_kernel, len(distances), len(at)), outs, places(at), spikes, down_w
        )
        return res[: len(distances)], res[len(distances) :]

    own, sib, fw, bw = scattered(down_blocks)
    emitted, current_grad, grad16 = call(
        functools.partial(out_kernel, steps, tokens),
        [((rows, local), bf16), ((rows, local), f32), ((rows, local), bf16)],
        own, sib, fw, bw, x, cot, out_threshold, out_width,
    )

    acc = None
    groups = gathered(grad16)
    for k, (pieces, at) in enumerate(groups):
        first, last = k == 0, k == len(groups) - 1
        args = [places(at), *pieces, down_w]
        aliases = {}
        if not first:
            if not last:
                aliases = {len(args): 0}
            args += [acc]
        outs = [((rows, hid), f32)]
        if last:
            args += [gate, upward, hid_level, hid_spread]
            outs = [((rows, hid), bf16)] * 2
        res = call(
            functools.partial(spike_grad_kernel, len(pieces), first, last, steps, tokens),
            outs,
            *args,
            aliases=aliases,
        )
        acc = res[0]
    gate_grad, up_grad = res

    def input_blocks(distances):
        at = [(d, s) for s in (False, True) for d in distances]
        outs = [((rows, local), bf16 if s else f32) for _, s in at]
        res = call(
            functools.partial(input_grad_kernel, len(at)),
            outs, places(at), gate_grad, up_grad, gate_w, up_w,
        )
        return res[: len(distances)], res[len(distances) :]

    own, sib, fw, bw = scattered(input_blocks)
    input_grad = (
        own + sib.astype(f32) + fw.astype(f32) + bw.astype(f32) + current_grad
    ).astype(bf16)

    sections = lax.axis_size("section")
    incoming = lax.ppermute(emitted, "section", [(s, s + 1) for s in range(sections - 1)])
    returned = lax.ppermute(input_grad, "section", [(s + 1, s) for s in range(sections - 1)])

    def viewed(v):
        return jnp.transpose(v.reshape(steps, tokens, local), (2, 0, 1))[None]

    return viewed(incoming), viewed(returned)


def solution(mesh):
    placed = (
        P("section", "dp", None, None),
        P("section", None, "dp"),
        P("section", None, "dp"),
        P("section", "dp", None),
        P("section", "dp"),
        P("section", "dp"),
        P("section", "dp"),
        P("section", "dp"),
        P("section", "dp", None, None),
    )
    return jax.shard_map(
        functools.partial(per_device, mesh.shape["dp"]),
        mesh=mesh,
        in_specs=placed,
        out_specs=(P("section", "dp", None, None), P("section", "dp", None, None)),
        check_vma=False,
    )
```

```python
import functools

import jax
import jax.numpy as jnp
from jax import lax
from jax.experimental import pallas as pl
from jax.experimental.pallas import tpu as pltpu
from jax.sharding import PartitionSpec as P

decay_rate = 0.9
level_unit = 0.125
f32 = jnp.float32
bf16 = jnp.bfloat16
VMEM_LIMIT = 8 * 1024 * 1024


def in_vmem(x):
    return pltpu.with_memory_space_constraint(x, pltpu.VMEM)


def call(kernel, outs, *args, flops=0, aliases=None, fetch=()):
    specs = []
    given = []
    for a in args:
        if a.dtype == jnp.int32 and a.ndim == 1:
            specs.append(pl.BlockSpec(memory_space=pltpu.SMEM))
            given.append(a)
        else:
            specs.append(pl.BlockSpec(memory_space=pltpu.VMEM))
            given.append(in_vmem(a))
    outs = list(outs)
    n_in, n_out, n_slabs, n_copies = len(args), len(outs), 0, 0
    for at, axis, local, weights in fetch:
        specs += [pl.BlockSpec(memory_space=pltpu.SMEM)] + [pl.BlockSpec(memory_space=pltpu.HBM)] * len(weights)
        given += [at] + [pltpu.with_memory_space_constraint(w, pltpu.HBM) for w in weights]
        for w in weights:
            size = at.shape[0] * local
            outs.append(((size, w.shape[1]) if axis == 0 else (w.shape[0], size), w.dtype))
        n_slabs += len(weights)
        n_copies += len(weights) * at.shape[0]

    def body(*refs):
        ins, refs = refs[:n_in], refs[n_in:]
        asked = []
        for at, axis, local, weights in fetch:
            asked.append((refs[0], refs[1 : 1 + len(weights)]))
            refs = refs[1 + len(weights) :]
        slabs = list(refs[n_out : n_out + n_slabs])
        copies = []
        for (at, axis, local, weights), (at_ref, sources) in zip(fetch, asked):
            mine, slabs = slabs[: len(weights)], slabs[len(weights) :]
            for p in range(at.shape[0]):
                here = pl.ds(pl.multiple_of(at_ref[p], local), local)
                there = slice(p * local, (p + 1) * local)
                for source, slab in zip(sources, mine):
                    pair = (
                        (source.at[here, :], slab.at[there, :])
                        if axis == 0
                        else (source.at[:, here], slab.at[:, there])
                    )
                    copies.append(pltpu.make_async_copy(*pair, refs[n_out + n_slabs].at[len(copies)]))
        for copy in copies:
            copy.start()
        if kernel is not None:
            kernel(*ins, *refs[:n_out])
        for copy in copies:
            copy.wait()

    res = pl.pallas_call(
        body,
        out_shape=[pltpu.VMEM(shape, dtype) for shape, dtype in outs],
        in_specs=specs,
        out_specs=[pl.BlockSpec(memory_space=pltpu.VMEM)] * len(outs),
        scratch_shapes=[pltpu.SemaphoreType.DMA((n_copies,))] if n_copies else [],
        input_output_aliases=aliases or {},
        compiler_params=pltpu.CompilerParams(vmem_limit_bytes=VMEM_LIMIT),
        cost_estimate=pl.CostEstimate(flops=flops, bytes_accessed=flops // 512, transcendentals=0),
    )(*given)
    slabs, got = list(res[n_out:]), []
    for _, _, _, weights in fetch:
        got.append(slabs[: len(weights)])
        slabs = slabs[len(weights) :]
    return list(res[:n_out]), got


def nn(left, right):
    return lax.dot_general(left, right, (((1,), (0,)), ((), ())), preferred_element_type=f32)


def nt(left, right):
    return lax.dot_general(left, right, (((1,), (1,)), ((), ())), preferred_element_type=f32)


def tiles(total, width):
    width = min(width, total)
    return [slice(k, k + width) for k in range(0, total, width)]


def levels(threshold_ref, width_ref, at):
    threshold = level_unit * threshold_ref[:, at].astype(f32)
    scale = 1.0 / (level_unit * width_ref[:, at].astype(f32))
    return threshold, scale


def spikes_of(currents, threshold, scale):
    potential = None
    out = []
    for current in currents:
        if potential is None:
            potential = current
        else:
            potential = decay_rate * (potential - threshold * out[-1]) + current
        out.append(jax.nn.sigmoid((potential - threshold) * scale))
    return out


def spikes_back(spikes, cotangents, threshold, scale):
    after = None
    grads = [None] * len(spikes)
    for t in reversed(range(len(spikes))):
        slope = spikes[t] * (1.0 - spikes[t]) * scale
        if after is None:
            after = cotangents[t] * slope
        else:
            after = (cotangents[t] - decay_rate * threshold * after) * slope + decay_rate * after
        grads[t] = after
    return grads


def tied(value, after):
    return value if after is None else lax.optimization_barrier((value, after))[0]


def step_rows(count, tokens):
    return [slice(t * tokens, (t + 1) * tokens) for t in range(count)]


def whole_pieces(refs, shape):
    out = []
    pending = None
    for ref in refs:
        if ref.shape == shape:
            out.append(ref[...])
        elif pending is None:
            pending = ref[...]
        else:
            out.append(jnp.concatenate([pending, ref[...]], axis=0))
            pending = None
    return out


def gate_up_kernel(n_pieces, first, last, steps, tokens, *refs):
    refs = list(refs)
    piece_refs, refs = refs[:n_pieces], refs[n_pieces:]
    slabs, refs = refs[:2], refs[2:]
    if not first:
        acc, refs = refs[:2], refs[2:]
    if last:
        threshold_ref, width_ref = refs[:2]
        refs = refs[2:]
    local = piece_refs[0].shape[1]
    left = jnp.concatenate(whole_pieces(piece_refs, (steps * tokens, local)), axis=1)
    for cols in tiles(refs[0].shape[1], 256):
        both = []
        for which in range(2):
            total = nn(left, slabs[which][:, cols])
            if not first:
                total = total + acc[which][:, cols]
            both.append(total)
            refs[which][:, cols] = total
        if last:
            threshold, scale = levels(threshold_ref, width_ref, cols)
            hidden = both[0] * jax.nn.sigmoid(both[0]) * both[1]
            parts = [hidden[r] for r in step_rows(steps, tokens)]
            out = spikes_of(parts, threshold, scale)
            refs[2][:, cols] = jnp.concatenate(out, axis=0).astype(bf16)


def down_kernel(spikes, slab, *outs):
    left = spikes[...]
    for p, out in enumerate(outs):
        local = out.shape[1]
        out[...] = nn(left, slab[:, p * local : (p + 1) * local]).astype(out.dtype)


def out_kernel(steps, tokens, own, sib, fw, bw, x, cot, threshold_ref, width_ref, emitted, grad, grad16):
    threshold, scale = levels(threshold_ref, width_ref, slice(None))
    current = (
        own[...] + sib[...].astype(f32) + fw[...].astype(f32) + bw[...].astype(f32) + x[...].astype(f32)
    )
    rows = step_rows(steps, tokens)
    out = spikes_of([current[r] for r in rows], threshold, scale)
    emitted[...] = jnp.concatenate(out, axis=0).astype(bf16)
    grads = spikes_back(out, [cot[r, :].astype(f32) for r in rows], threshold, scale)
    total = jnp.concatenate(grads, axis=0)
    grad[...] = total
    grad16[...] = total.astype(bf16)


def spike_grad_kernel(n_pieces, first, last, steps, tokens, *refs):
    refs = list(refs)
    piece_refs, refs = refs[:n_pieces], refs[n_pieces:]
    slab, refs = refs[0], refs[1:]
    if not first:
        acc, refs = refs[0], refs[1:]
    if last:
        gate, up, threshold_ref, width_ref = refs[:4]
        refs = refs[4:]
    local = piece_refs[0].shape[1]
    left = jnp.concatenate(whole_pieces(piece_refs, (steps * tokens, local)), axis=1)
    for hid in tiles(slab.shape[0], 256):
        total = nt(left, slab[hid, :])
        if not first:
            total = total + acc[:, hid]
        if not last:
            refs[0][:, hid] = total
            continue
        threshold, scale = levels(threshold_ref, width_ref, hid)
        gate_in, up_in = gate[:, hid], up[:, hid]
        sig = jax.nn.sigmoid(gate_in)
        act = gate_in * sig
        hidden = act * up_in
        parts = step_rows(steps, tokens)
        out = spikes_of([hidden[r] for r in parts], threshold, scale)
        grads = spikes_back(out, [total[r] for r in parts], threshold, scale)
        grad = jnp.concatenate(grads, axis=0)
        refs[0][:, hid] = (grad * up_in * (sig * (1.0 + gate_in * (1.0 - sig)))).astype(bf16)
        refs[1][:, hid] = (grad * act).astype(bf16)


def input_grad_kernel(gate_grad, up_grad, gate_slab, up_slab, *outs):
    left = jnp.concatenate([gate_grad[...], up_grad[...]], axis=1)
    for p, out in enumerate(outs):
        local = out.shape[1]
        here = slice(p * local, (p + 1) * local)
        right = jnp.concatenate([gate_slab[here, :], up_slab[here, :]], axis=1)
        out[...] = nt(left, right).astype(out.dtype)


def per_device(
    devices,
    layer_input,
    gate_weight,
    up_weight,
    down_weight,
    hidden_threshold,
    hidden_width,
    out_threshold,
    out_width,
    out_cotangent,
):
    local = layer_input.shape[1]
    steps = layer_input.shape[2]
    tokens = layer_input.shape[3]
    rows = steps * tokens
    half = rows // 2
    hid = gate_weight.shape[2]
    chips = devices // 2
    far = chips // 2
    side = chips // 2

    def chip_at(place):
        place = place % chips
        return jnp.where(place < side, 2 * place, 2 * (chips - 1 - place) + 1)

    order = [2 * p if p < side else 2 * (chips - 1 - p) + 1 for p in range(chips)]
    forward, backward, sibling = [], [], []
    for p in range(chips):
        a, b = order[p], order[(p + 1) % chips]
        for core in range(2):
            forward.append((2 * a + core, 2 * b + core))
            backward.append((2 * b + core, 2 * a + core))
            sibling.append((2 * a + core, 2 * a + 1 - core))
    send_fw = lambda v: lax.ppermute(v, "dp", forward)
    send_bw = lambda v: lax.ppermute(v, "dp", backward)
    swap = lambda v: lax.ppermute(v, "dp", sibling)

    index = lax.axis_index("dp").astype(jnp.int32)
    chip, core = index // 2, index % 2
    place = jnp.where(chip % 2 == 0, chip // 2, chips - 1 - chip // 2)

    def block_at(distance, sib):
        which = 2 * chip_at(place + distance) + (1 - core if sib else core)
        return which * local

    x = jnp.transpose(layer_input[0], (1, 2, 0)).reshape(rows, local)
    cot = jnp.transpose(out_cotangent[0], (1, 2, 0)).reshape(rows, local)

    def with_sibling(distances):
        return [(d, s) for s in (False, True) for d in distances]

    come = [[0]] + [[-k, k] for k in range(1, far)] + [[-far]]
    gathers = [
        [(d, False) for d in now] + [(d, True) for d in before]
        for now, before in zip(come + [[]], [[]] + come)
    ]
    scatters = [with_sibling(g) for g in [[far]] + [[k, -k] for k in range(far - 1, 0, -1)] + [[0]]]
    gate_up = (0, local, (gate_weight[0], up_weight[0]))
    down = (1, local, (down_weight[0],))
    phases = ((gathers, gate_up), (scatters, down), (gathers, down), (scatters, gate_up))
    wanted = {(f, k): (g, *w) for f, (gs, w) in enumerate(phases) for k, g in enumerate(gs)}
    end = far + 1
    brought_by = {(0, 0): [(0, 1), (0, 2)], (1, far): [(2, 0), (2, 1)], (2, 0): [(2, 2), (2, 3)]}
    for k in range(1, far):
        brought_by[0, k] = [(0, k + 2)]
        brought_by[2, k] = [(2, k + 3)] if k + 3 <= end else []
    brought_by[0, far - 2] = [(0, far), (0, end)]
    brought_by[0, far - 1] = [(1, 0), (1, 1)]
    brought_by[2, far - 2] = [(2, far), (2, end), (3, 0)]
    if far > 2:
        brought_by[2, far - 1] = [(3, 1)]
    held_slabs = {}

    def bring(which, after=None):
        group, axis, size, weights = wanted[which]
        at = jnp.stack([block_at(d, s) for d, s in group]).astype(jnp.int32)
        return (tied(at, after), axis, size, weights)

    def run(which, kernel, outs, *args, after=None, **kwargs):
        if which not in held_slabs:
            held_slabs[which] = call(None, [], fetch=[bring(which, after)])[1][0]
        given = []
        for a in args:
            given += held_slabs[which] if a is None else [a]
        later = brought_by.get(which, [])
        if which[0] in (1, 3) and 1 <= which[1] < far and (which[0], which[1] + 1) not in later:
            later = later + [(which[0], which[1] + 1)]
        later = [w for w in later if w not in held_slabs]
        res, got = call(kernel, outs, *given, fetch=[bring(w, after) for w in later], **kwargs)
        held_slabs.update(zip(later, got))
        return res

    def gathered(mine, take):
        own, sib, held = [mine], [], None
        fw = bw = mine
        for k in range(1, far + 1):
            sent = (fw[:half], bw[half:]) if k == far else (fw, bw)
            fw, bw = send_fw(sent[0]), send_bw(sent[1])
            swaps = [swap(v) for v in own]
            held = take(own + sib, k - 1, held)
            sib = swaps
            fw, bw, held = lax.optimization_barrier((fw, bw, held))
            own = [fw, bw]
        swaps = [swap(v) for v in own]
        held = take(own + sib, far, held)
        return take(swaps, far + 1, held)

    def scattered(blocks_of):
        def summed(blocks, swaps):
            return [o + s.astype(f32) for o, s in zip(blocks[0], swaps)]

        now = blocks_of(0, None)
        swaps = [swap(v) for v in now[1]]
        later = blocks_of(1, None)
        now, swaps, later = lax.optimization_barrier((now, swaps, later))
        total = summed(now, swaps)[0]
        fw, bw = total[:half].astype(bf16), total[half:].astype(bf16)
        for k in range(1, far):
            after = fw
            fw, bw = send_fw(fw), send_bw(bw)
            now = later
            swaps = [swap(v) for v in now[1]]
            later = blocks_of(k + 1, after)
            fw, bw, later = lax.optimization_barrier((fw, bw, later))
            a, b = summed(now, swaps)
            if k == 1:
                fw = jnp.concatenate([a[:half] + fw.astype(f32), a[half:]], axis=0).astype(bf16)
                bw = jnp.concatenate([b[:half], b[half:] + bw.astype(f32)], axis=0).astype(bf16)
            else:
                fw, bw = (a + fw.astype(f32)).astype(bf16), (b + bw.astype(f32)).astype(bf16)
        fw, bw = send_fw(fw), send_bw(bw)
        return later[0][0], swap(later[1][0]), fw, bw

    hid_level, hid_spread = hidden_threshold, hidden_width

    def take_inputs(pieces, k, acc):
        first, last = k == 0, k == end
        args = [*pieces, None]
        aliases = {}
        if not first:
            aliases = {len(pieces) + 2: 0, len(pieces) + 3: 1}
            args += list(acc)
        outs = [((rows, hid), f32)] * 2
        if last:
            args += [hid_level, hid_spread]
            outs = outs + [((rows, hid), bf16)]
        return run(
            (0, k),
            functools.partial(gate_up_kernel, len(pieces), first, last, steps, tokens),
            outs,
            *args,
            flops=4 * rows * hid * local * len(gathers[k]),
            aliases=aliases,
            after=x if first else None,
        )

    gate, upward, spikes = gathered(x, take_inputs)

    def down_blocks(k, after):
        outs = [((rows, local), bf16 if s else f32) for _, s in scatters[k]]
        res = run(
            (1, k), down_kernel, outs, spikes, None,
            flops=2 * rows * hid * local * len(outs), after=after,
        )
        return res[: len(res) // 2], res[len(res) // 2 :]

    own, sib, fw, bw = scattered(down_blocks)
    (emitted, current_grad, grad16), _ = call(
        functools.partial(out_kernel, steps, tokens),
        [((rows, local), bf16), ((rows, local), f32), ((rows, local), bf16)],
        own, sib, fw, bw, x, cot, out_threshold, out_width,
    )

    def take_grads(pieces, k, acc):
        first, last = k == 0, k == end
        args = [*pieces, None]
        aliases = {}
        if not first:
            if not last:
                aliases = {len(pieces) + 1: 0}
            args += acc
        outs = [((rows, hid), f32)]
        if last:
            args += [gate, upward, hid_level, hid_spread]
            outs = [((rows, hid), bf16)] * 2
        return run(
            (2, k),
            functools.partial(spike_grad_kernel, len(pieces), first, last, steps, tokens),
            outs,
            *args,
            flops=2 * rows * hid * local * len(gathers[k]),
            aliases=aliases,
        )

    gate_grad, up_grad = gathered(grad16, take_grads)

    def input_blocks(k, after):
        outs = [((rows, local), bf16 if s else f32) for _, s in scatters[k]]
        res = run(
            (3, k), input_grad_kernel, outs, gate_grad, up_grad, None,
            flops=4 * rows * hid * local * len(outs), after=after,
        )
        return res[: len(res) // 2], res[len(res) // 2 :]

    own, sib, fw, bw = scattered(input_blocks)
    input_grad = (
        own + sib.astype(f32) + fw.astype(f32) + bw.astype(f32) + current_grad
    ).astype(bf16)

    sections = lax.axis_size("section")
    incoming = lax.ppermute(emitted, "section", [(s, s + 1) for s in range(sections - 1)])
    returned = lax.ppermute(input_grad, "section", [(s + 1, s) for s in range(sections - 1)])

    def viewed(v):
        return jnp.transpose(v.reshape(steps, tokens, local), (2, 0, 1))[None]

    return viewed(incoming), viewed(returned)


def solution(mesh):
    placed = (
        P("section", "dp", None, None),
        P("section", None, "dp"),
        P("section", None, "dp"),
        P("section", "dp", None),
        P("section", "dp"),
        P("section", "dp"),
        P("section", "dp"),
        P("section", "dp"),
        P("section", "dp", None, None),
    )
    return jax.shard_map(
        functools.partial(per_device, mesh.shape["dp"]),
        mesh=mesh,
        in_specs=placed,
        out_specs=(P("section", "dp", None, None), P("section", "dp", None, None)),
        check_vma=False,
    )
```

```python
import functools

import jax
import jax.numpy as jnp
from jax import lax
from jax.experimental import pallas as pl
from jax.experimental.pallas import tpu as pltpu
from jax.sharding import PartitionSpec as P

decay_rate = 0.9
level_unit = 0.125
f32 = jnp.float32
bf16 = jnp.bfloat16
VMEM_LIMIT = 8 * 1024 * 1024


def in_vmem(x):
    return pltpu.with_memory_space_constraint(x, pltpu.VMEM)


def call(kernel, outs, *args, flops=0, aliases=None, fetch=()):
    specs = []
    given = []
    for a in args:
        if a.dtype == jnp.int32 and a.ndim == 1:
            specs.append(pl.BlockSpec(memory_space=pltpu.SMEM))
            given.append(a)
        else:
            specs.append(pl.BlockSpec(memory_space=pltpu.VMEM))
            given.append(in_vmem(a))
    n_in, n_out, n_fetch = len(args), len(outs), len(fetch)
    specs += [pl.BlockSpec(memory_space=pltpu.HBM)] * n_fetch
    given += [pltpu.with_memory_space_constraint(w, pltpu.HBM) for w in fetch]
    outs = list(outs) + [(w.shape, w.dtype) for w in fetch]

    def body(*refs):
        ins, sources, refs = refs[:n_in], refs[n_in : n_in + n_fetch], refs[n_in + n_fetch :]
        copies = [
            pltpu.make_async_copy(sources[w], refs[n_out + w], refs[n_out + n_fetch].at[w])
            for w in range(n_fetch)
        ]
        for copy in copies:
            copy.start()
        if kernel is not None:
            kernel(*ins, *refs[:n_out])
        for copy in copies:
            copy.wait()

    res = pl.pallas_call(
        body,
        out_shape=[pltpu.VMEM(shape, dtype) for shape, dtype in outs],
        in_specs=specs,
        out_specs=[pl.BlockSpec(memory_space=pltpu.VMEM)] * len(outs),
        scratch_shapes=[pltpu.SemaphoreType.DMA((n_fetch,))] if n_fetch else [],
        input_output_aliases=aliases or {},
        compiler_params=pltpu.CompilerParams(vmem_limit_bytes=VMEM_LIMIT),
        cost_estimate=pl.CostEstimate(flops=flops, bytes_accessed=flops // 512, transcendentals=0),
    )(*given)
    return list(res[:n_out]), list(res[n_out:])


def nn(left, right):
    return lax.dot_general(left, right, (((1,), (0,)), ((), ())), preferred_element_type=f32)


def nt(left, right):
    return lax.dot_general(left, right, (((1,), (1,)), ((), ())), preferred_element_type=f32)


def tiles(total, width):
    width = min(width, total)
    return [slice(k, k + width) for k in range(0, total, width)]


def levels(threshold_ref, width_ref, at):
    threshold = level_unit * threshold_ref[:, at].astype(f32)
    scale = 1.0 / (level_unit * width_ref[:, at].astype(f32))
    return threshold, scale


def sigmoid(v):
    return 0.5 * jnp.tanh(0.5 * v) + 0.5


def spikes_of(currents, threshold, scale):
    potential = None
    out = []
    for current in currents:
        if potential is None:
            potential = current
        else:
            potential = decay_rate * (potential - threshold * out[-1]) + current
        out.append(sigmoid((potential - threshold) * scale))
    return out


def slopes_of(spikes, scale):
    return [v * (1.0 - v) * scale for v in spikes]


def spikes_back(slopes, cotangents, threshold):
    after = None
    grads = [None] * len(slopes)
    for t in reversed(range(len(slopes))):
        if after is None:
            after = cotangents[t] * slopes[t]
        else:
            after = (cotangents[t] - decay_rate * threshold * after) * slopes[t] + decay_rate * after
        grads[t] = after
    return grads


def tied(value, after):
    return lax.optimization_barrier((value, after))[0]


def step_rows(count, tokens):
    return [slice(t * tokens, (t + 1) * tokens) for t in range(count)]


def whole_pieces(refs, shape):
    out = []
    pending = None
    for ref in refs:
        if ref.shape == shape:
            out.append(ref[...])
        elif pending is None:
            pending = ref[...]
        else:
            out.append(jnp.concatenate([pending, ref[...]], axis=0))
            pending = None
    return out


def block_of(spot, local, chips):
    index = lax.axis_index("dp")
    chip, core = index // 2, index % 2
    side = chips // 2
    place = jnp.where(chip % 2 == 0, chip // 2, chips - 1 - chip // 2)
    place = (place + spot // 2) % chips
    chip = jnp.where(place < side, 2 * place, 2 * (chips - 1 - place) + 1)
    core = 1 - core if spot % 2 else core
    return pl.ds(pl.multiple_of((2 * chip + core) * local, local), local)


def turn_kernel(raw, out):
    tokens = raw.shape[2]
    for t in range(raw.shape[1]):
        out[t * tokens : (t + 1) * tokens, :] = raw[:, t, :].astype(f32).T.astype(out.dtype)


def turned(raw):
    shape = (raw.shape[1] * raw.shape[2], raw.shape[0])
    return call(turn_kernel, [(shape, raw.dtype)], raw)[0][0]


def gate_up_kernel(chips, spots, n_pieces, first, last, steps, tokens, *refs):
    refs = list(refs)
    piece_refs, refs = refs[:n_pieces], refs[n_pieces:]
    weights, refs = refs[:2], refs[2:]
    if not first:
        acc, refs = refs[:2], refs[2:]
    if last:
        threshold_ref, width_ref = refs[:2]
        refs = refs[2:]
    local = piece_refs[0].shape[1]
    left = jnp.concatenate(whole_pieces(piece_refs, (steps * tokens, local)), axis=1)
    blocks = [block_of(p, local, chips) for p in spots]
    for cols in tiles(refs[0].shape[1], 256):
        both = []
        for which in range(2):
            right = jnp.concatenate([weights[which][here, cols] for here in blocks], axis=0)
            total = nn(left, right)
            if not first:
                total = total + acc[which][:, cols]
            both.append(total)
            refs[which][:, cols] = total
        if last:
            threshold, scale = levels(threshold_ref, width_ref, cols)
            hidden = both[0] * sigmoid(both[0]) * both[1]
            parts = [hidden[r] for r in step_rows(steps, tokens)]
            out = spikes_of(parts, threshold, scale)
            refs[2][:, cols] = jnp.concatenate(out, axis=0).astype(bf16)


def down_kernel(chips, spots, spikes, down, *outs):
    left = spikes[...]
    for p, out in zip(spots, outs):
        out[...] = nn(left, down[:, block_of(p, out.shape[1], chips)]).astype(out.dtype)


def out_kernel(steps, tokens, own, sib, fw, bw, x, cot, threshold_ref, width_ref, emitted, grad, grad16):
    threshold, scale = levels(threshold_ref, width_ref, slice(None))
    current = (
        own[...] + sib[...].astype(f32) + fw[...].astype(f32) + bw[...].astype(f32) + x[...].astype(f32)
    )
    rows = step_rows(steps, tokens)
    out = spikes_of([current[r] for r in rows], threshold, scale)
    emitted[...] = jnp.concatenate(out, axis=0).astype(bf16)
    grads = spikes_back(slopes_of(out, scale), [cot[r, :].astype(f32) for r in rows], threshold)
    total = jnp.concatenate(grads, axis=0)
    grad[...] = total
    grad16[...] = total.astype(bf16)


def spike_grad_kernel(chips, spots, n_pieces, first, last, steps, tokens, *refs):
    refs = list(refs)
    piece_refs, refs = refs[:n_pieces], refs[n_pieces:]
    down, refs = refs[0], refs[1:]
    if not first:
        acc, refs = refs[0], refs[1:]
    if last:
        slope, to_gate, to_up, threshold_ref, width_ref = refs[:5]
        refs = refs[5:]
    local = piece_refs[0].shape[1]
    left = jnp.concatenate(whole_pieces(piece_refs, (steps * tokens, local)), axis=1)
    blocks = [block_of(p, local, chips) for p in spots]
    for hid in tiles(down.shape[0], 256):
        total = nt(left, jnp.concatenate([down[hid, here] for here in blocks], axis=1))
        if not first:
            total = total + acc[:, hid]
        if not last:
            refs[0][:, hid] = total
            continue
        threshold, _ = levels(threshold_ref, width_ref, hid)
        parts = step_rows(steps, tokens)
        grads = spikes_back([slope[r, hid] for r in parts], [total[r] for r in parts], threshold)
        grad = jnp.concatenate(grads, axis=0)
        refs[0][:, hid] = (grad * to_gate[:, hid]).astype(bf16)
        refs[1][:, hid] = (grad * to_up[:, hid]).astype(bf16)


def slopes_kernel(steps, tokens, gate, up, threshold_ref, width_ref, slope, to_gate, to_up):
    for hid in tiles(gate.shape[1], 256):
        threshold, scale = levels(threshold_ref, width_ref, hid)
        gate_in, up_in = gate[:, hid], up[:, hid]
        sig = sigmoid(gate_in)
        act = gate_in * sig
        hidden = act * up_in
        parts = step_rows(steps, tokens)
        out = spikes_of([hidden[r] for r in parts], threshold, scale)
        slope[:, hid] = jnp.concatenate(slopes_of(out, scale), axis=0)
        to_gate[:, hid] = up_in * (sig * (1.0 + gate_in * (1.0 - sig)))
        to_up[:, hid] = act


def input_grad_kernel(chips, spots, gate_grad, up_grad, gate_w, up_w, *outs):
    left = jnp.concatenate([gate_grad[...], up_grad[...]], axis=1)
    for p, out in zip(spots, outs):
        here = block_of(p, out.shape[1], chips)
        right = jnp.concatenate([gate_w[here, :], up_w[here, :]], axis=1)
        out[...] = nt(left, right).astype(out.dtype)


def per_device(
    devices,
    layer_input,
    gate_weight,
    up_weight,
    down_weight,
    hidden_threshold,
    hidden_width,
    out_threshold,
    out_width,
    out_cotangent,
):
    local = layer_input.shape[1]
    steps = layer_input.shape[2]
    tokens = layer_input.shape[3]
    rows = steps * tokens
    half = rows // 2
    hid = gate_weight.shape[2]
    chips = devices // 2
    far = chips // 2
    side = chips // 2

    order = [2 * p if p < side else 2 * (chips - 1 - p) + 1 for p in range(chips)]
    forward, backward, sibling = [], [], []
    for p in range(chips):
        a, b = order[p], order[(p + 1) % chips]
        for core in range(2):
            forward.append((2 * a + core, 2 * b + core))
            backward.append((2 * b + core, 2 * a + core))
            sibling.append((2 * a + core, 2 * a + 1 - core))
    send_fw = lambda v: lax.ppermute(v, "dp", forward)
    send_bw = lambda v: lax.ppermute(v, "dp", backward)
    swap = lambda v: lax.ppermute(v, "dp", sibling)

    x = turned(layer_input[0])
    cot = turned(out_cotangent[0])

    gate_hbm, up_hbm, down_hbm = gate_weight[0], up_weight[0], down_weight[0]
    spots = lambda at: [(d % chips) * 2 + s for d, s in at]

    def gathered(mine, take, beside):
        held, own, sib = None, [], []
        fw = bw = mine

        def taken(new, last=False):
            pieces = [p for v, _ in new for p in (v if isinstance(v, tuple) else (v,))]
            return take(pieces, [at for _, at in new], held, last)

        def swapped(new):
            return [
                (tuple(map(swap, v)) if isinstance(v, tuple) else swap(v), (d, True)) for v, (d, _) in new
            ]

        for k in range(1, far + 1):
            sent = (fw[:half], bw[half:]) if k == far else (fw, bw)
            next_fw, next_bw = send_fw(sent[0]), send_bw(sent[1])
            if k == 1:
                own = [(mine, (0, False))]
                sib = own + swapped(own)
            else:
                own = [(fw, (1 - k, False)), (bw, (k - 1, False))]
                held, sib = taken(own + sib), swapped(own)
            fw, bw = next_fw, next_bw
            fw, held, _ = lax.optimization_barrier((fw, held, beside.get(k)))
            bw = tied(bw, held)
        own = [((fw, bw), (-far, False))]
        last = swapped(own)
        held = taken(own + sib)
        return taken(last, last=True)

    def scattered(blocks_of, parts):
        def group(k):
            return [(d, s) for s in (False, True) for d in ([k, -k] if k else [0])]

        def sums(own, sib):
            return [o + s.astype(f32) for o, s in zip(own, sib)]

        sib = swap(blocks_of([(far, True)], None)[0])
        first = blocks_of([(far, False)] + group(far - 1)[2:], None)
        total = first[0] + sib.astype(f32)
        fw, bw = total[:half].astype(bf16), total[half:].astype(bf16)
        now_sib, now_own = first[1:], None
        cut = [slice(p * rows // parts, (p + 1) * rows // parts) for p in range(parts)]
        for k in range(1, far):
            after = fw
            fw, bw = send_fw(fw), send_bw(bw)
            now_sib = [swap(v) for v in now_sib]
            if k == 1:
                later = blocks_of(group(far - 1)[:2] + group(far - 2), after)
                now_own, later = later[:2], later[2:]
            else:
                later = blocks_of(group(far - k - 1), after)
            fw, later = lax.optimization_barrier((fw, later))
            bw = tied(bw, later)
            a, b = sums(now_own, now_sib)
            if k == 1:
                fw = jnp.concatenate([a[:half] + fw.astype(f32), a[half:]], axis=0).astype(bf16)
                bw = jnp.concatenate([b[:half], b[half:] + bw.astype(f32)], axis=0).astype(bf16)
            else:
                fw, bw = (a + fw.astype(f32)).astype(bf16), (b + bw.astype(f32)).astype(bf16)
            now_own, now_sib = later[: len(later) // 2], later[len(later) // 2 :]
        ends = [(send_fw(fw[c]), send_bw(bw[c])) for c in cut]
        return now_own[0], swap(now_sib[0]), [e[0] for e in ends], [e[1] for e in ends], cut

    hid_level, hid_spread = hidden_threshold, hidden_width
    gate_w, up_w = call(None, [], fetch=(tied(gate_hbm, x), up_hbm))[1]
    down_w = None

    def take_inputs(pieces, at, acc, last):
        nonlocal down_w
        first = acc is None
        args = [*pieces, gate_w, up_w]
        aliases = {}
        if not first:
            aliases = {len(args): 0, len(args) + 1: 1}
            args += list(acc)
        outs = [((rows, hid), f32)] * 2
        if last:
            args += [hid_level, hid_spread]
            outs = outs + [((rows, hid), bf16)]
        res, new = call(
            functools.partial(gate_up_kernel, chips, spots(at), len(pieces), first, last, steps, tokens),
            outs,
            *args,
            flops=4 * rows * hid * local * len(at),
            aliases=aliases,
            fetch=(down_hbm,) if first else (),
        )
        if new:
            down_w = new[0]
        return res

    gate, upward, spikes = gathered(x, take_inputs, {1: (gate_w, up_w)})

    def blocks(kernel, flops, *args):
        def blocks_of(at, after):
            outs = [((rows, local), bf16 if s else f32) for _, s in at]
            first = args[0] if after is None else tied(args[0], after)
            return call(functools.partial(kernel, chips, spots(at)), outs, first, *args[1:], flops=len(at) * flops)[0]

        return blocks_of

    own, sib, fw, bw, _ = scattered(blocks(down_kernel, 2 * rows * hid * local, spikes, down_w), 1)
    (emitted, current_grad, grad16), _ = call(
        functools.partial(out_kernel, steps, tokens),
        [((rows, local), bf16), ((rows, local), f32), ((rows, local), bf16)],
        own, sib, fw[0], bw[0], x, cot, out_threshold, out_width,
    )

    sections = lax.axis_size("section")
    incoming = lax.ppermute(emitted, "section", [(s, s + 1) for s in range(sections - 1)])
    way_back, _ = call(
        functools.partial(slopes_kernel, steps, tokens),
        [((rows, hid), f32)] * 3,
        tied(gate, grad16), upward, hid_level, hid_spread,
        flops=2 * rows * hid * local,
    )

    def take_grads(pieces, at, acc, last):
        first = acc is None
        args = [*pieces, down_w]
        aliases = {}
        if not first:
            if not last:
                aliases = {len(args): 0}
            args += acc
        outs = [((rows, hid), f32)]
        if last:
            args += [*way_back, hid_level, hid_spread]
            outs = [((rows, hid), bf16)] * 2
        return call(
            functools.partial(spike_grad_kernel, chips, spots(at), len(pieces), first, last, steps, tokens),
            outs,
            *args,
            flops=2 * rows * hid * local * len(at),
            aliases=aliases,
        )[0]

    gate_grad, up_grad = gathered(grad16, take_grads, {1: way_back, 2: incoming})

    own, sib, fw, bw, cut = scattered(
        blocks(input_grad_kernel, 4 * rows * hid * local, gate_grad, up_grad, gate_w, up_w), 2
    )
    returned = []
    for c, from_fw, from_bw in zip(cut, fw, bw):
        total = own[c] + sib[c].astype(f32) + current_grad[c] + from_fw.astype(f32) + from_bw.astype(f32)
        returned.append(
            lax.ppermute(total.astype(bf16), "section", [(s + 1, s) for s in range(sections - 1)])
        )

    def viewed(v):
        return jnp.transpose(v.reshape(steps, tokens, local), (2, 0, 1))[None]

    return viewed(incoming), viewed(jnp.concatenate(returned, axis=0))


def solution(mesh):
    placed = (
        P("section", "dp", None, None),
        P("section", None, "dp"),
        P("section", None, "dp"),
        P("section", "dp", None),
        P("section", "dp"),
        P("section", "dp"),
        P("section", "dp"),
        P("section", "dp"),
        P("section", "dp", None, None),
    )
    return jax.shard_map(
        functools.partial(per_device, mesh.shape["dp"]),
        mesh=mesh,
        in_specs=placed,
        out_specs=(P("section", "dp", None, None), P("section", "dp", None, None)),
        check_vma=False,
    )
```

```python
import functools

import jax
import jax.numpy as jnp
from jax import lax
from jax.experimental import pallas as pl
from jax.experimental.pallas import tpu as pltpu
from jax.sharding import PartitionSpec as P

decay_rate = 0.9
level_unit = 0.125
f32 = jnp.float32
bf16 = jnp.bfloat16
VMEM_LIMIT = 8 * 1024 * 1024


def in_vmem(x):
    return pltpu.with_memory_space_constraint(x, pltpu.VMEM)


def call(kernel, outs, *args, flops=0, aliases=None, fetch=()):
    specs = []
    given = []
    for a in args:
        if a.dtype == jnp.int32 and a.ndim == 1:
            specs.append(pl.BlockSpec(memory_space=pltpu.SMEM))
            given.append(a)
        else:
            specs.append(pl.BlockSpec(memory_space=pltpu.VMEM))
            given.append(in_vmem(a))
    n_in, n_out, n_fetch = len(args), len(outs), len(fetch)
    specs += [pl.BlockSpec(memory_space=pltpu.HBM)] * n_fetch
    given += [pltpu.with_memory_space_constraint(w, pltpu.HBM) for w in fetch]
    outs = list(outs) + [(w.shape, w.dtype) for w in fetch]

    def body(*refs):
        ins, sources, refs = refs[:n_in], refs[n_in : n_in + n_fetch], refs[n_in + n_fetch :]
        copies = [
            pltpu.make_async_copy(sources[w], refs[n_out + w], refs[n_out + n_fetch].at[w])
            for w in range(n_fetch)
        ]
        for copy in copies:
            copy.start()
        if kernel is not None:
            kernel(*ins, *refs[:n_out])
        for copy in copies:
            copy.wait()

    res = pl.pallas_call(
        body,
        out_shape=[pltpu.VMEM(shape, dtype) for shape, dtype in outs],
        in_specs=specs,
        out_specs=[pl.BlockSpec(memory_space=pltpu.VMEM)] * len(outs),
        scratch_shapes=[pltpu.SemaphoreType.DMA((n_fetch,))] if n_fetch else [],
        input_output_aliases=aliases or {},
        compiler_params=pltpu.CompilerParams(vmem_limit_bytes=VMEM_LIMIT),
        cost_estimate=pl.CostEstimate(flops=max(flops, 1), bytes_accessed=max(flops // 512, 1), transcendentals=0),
    )(*given)
    return list(res[:n_out]), list(res[n_out:])


def nn(left, right):
    return lax.dot_general(left, right, (((1,), (0,)), ((), ())), preferred_element_type=f32)


def nt(left, right):
    return lax.dot_general(left, right, (((1,), (1,)), ((), ())), preferred_element_type=f32)


def over_tiles(total, width, work):
    width = min(width, total)

    def body(k, carry):
        work(pl.ds(pl.multiple_of(k * width, width), width))
        return carry

    lax.fori_loop(0, total // width, body, 0)


def levels(threshold_ref, width_ref, at):
    threshold = level_unit * threshold_ref[:, at].astype(f32)
    scale = 1.0 / (level_unit * width_ref[:, at].astype(f32))
    return threshold, scale


def sigmoid(v):
    return 0.5 * jnp.tanh(0.5 * v) + 0.5


def spikes_of(currents, threshold, scale):
    potential = None
    out = []
    for current in currents:
        if potential is None:
            potential = current
        else:
            potential = decay_rate * (potential - threshold * out[-1]) + current
        out.append(sigmoid((potential - threshold) * scale))
    return out


def slopes_of(spikes, scale):
    return [v * (1.0 - v) * scale for v in spikes]


def spikes_back(slopes, cotangents, threshold):
    after = None
    grads = [None] * len(slopes)
    for t in reversed(range(len(slopes))):
        if after is None:
            after = cotangents[t] * slopes[t]
        else:
            after = (cotangents[t] - decay_rate * threshold * after) * slopes[t] + decay_rate * after
        grads[t] = after
    return grads


def tied(value, after):
    return lax.optimization_barrier((value, after))[0]


def step_rows(count, tokens):
    return [slice(t * tokens, (t + 1) * tokens) for t in range(count)]


def whole_pieces(refs, shape):
    out = []
    pending = None
    for ref in refs:
        if ref.shape == shape:
            out.append(ref[...])
        elif pending is None:
            pending = ref[...]
        else:
            out.append(jnp.concatenate([pending, ref[...]], axis=0))
            pending = None
    return out


def block_of(spot, local, chips):
    index = lax.axis_index("dp")
    chip, core = index // 2, index % 2
    side = chips // 2
    place = jnp.where(chip % 2 == 0, chip // 2, chips - 1 - chip // 2)
    place = (place + spot // 2) % chips
    chip = jnp.where(place < side, 2 * place, 2 * (chips - 1 - place) + 1)
    core = 1 - core if spot % 2 else core
    return pl.ds(pl.multiple_of((2 * chip + core) * local, local), local)


def turn_kernel(raw, out):
    tokens = raw.shape[2]
    for t in range(raw.shape[1]):
        out[t * tokens : (t + 1) * tokens, :] = raw[:, t, :].astype(f32).T.astype(out.dtype)


def turned(raw):
    shape = (raw.shape[1] * raw.shape[2], raw.shape[0])
    return call(turn_kernel, [(shape, raw.dtype)], raw)[0][0]


def gate_up_kernel(chips, spots, n_pieces, first, last, steps, tokens, *refs):
    refs = list(refs)
    piece_refs, refs = refs[:n_pieces], refs[n_pieces:]
    weights, refs = refs[:2], refs[2:]
    if not first:
        acc, refs = refs[:2], refs[2:]
    if last:
        threshold_ref, width_ref = refs[:2]
        refs = refs[2:]
    local = piece_refs[0].shape[1]
    blocks = [block_of(p, local, chips) for p in spots]

    def work(cols):
        left = jnp.concatenate(whole_pieces(piece_refs, (steps * tokens, local)), axis=1)
        both = []
        for which in range(2):
            right = jnp.concatenate([weights[which][here, cols] for here in blocks], axis=0)
            total = nn(left, right)
            if not first:
                total = total + acc[which][:, cols]
            both.append(total)
            refs[which][:, cols] = total
        if last:
            threshold, scale = levels(threshold_ref, width_ref, cols)
            hidden = both[0] * sigmoid(both[0]) * both[1]
            parts = [hidden[r] for r in step_rows(steps, tokens)]
            out = spikes_of(parts, threshold, scale)
            refs[2][:, cols] = jnp.concatenate(out, axis=0).astype(bf16)

    over_tiles(refs[0].shape[1], 512, work)


def down_kernel(chips, spots, spikes, down, *outs):
    left = spikes[...]
    for p, out in zip(spots, outs):
        out[...] = nn(left, down[:, block_of(p, out.shape[1], chips)]).astype(out.dtype)


def out_kernel(steps, tokens, own, sib, fw, bw, x, cot, threshold_ref, width_ref, emitted, grad, grad16):
    threshold, scale = levels(threshold_ref, width_ref, slice(None))
    current = (
        own[...] + sib[...].astype(f32) + fw[...].astype(f32) + bw[...].astype(f32) + x[...].astype(f32)
    )
    rows = step_rows(steps, tokens)
    out = spikes_of([current[r] for r in rows], threshold, scale)
    emitted[...] = jnp.concatenate(out, axis=0).astype(bf16)
    grads = spikes_back(slopes_of(out, scale), [cot[r, :].astype(f32) for r in rows], threshold)
    total = jnp.concatenate(grads, axis=0)
    grad[...] = total
    grad16[...] = total.astype(bf16)


def spike_grad_kernel(chips, spots, n_pieces, first, last, steps, tokens, *refs):
    refs = list(refs)
    piece_refs, refs = refs[:n_pieces], refs[n_pieces:]
    down, refs = refs[0], refs[1:]
    if not first:
        acc, refs = refs[0], refs[1:]
    if last:
        slope, to_gate, to_up, threshold_ref, width_ref = refs[:5]
        refs = refs[5:]
    local = piece_refs[0].shape[1]
    blocks = [block_of(p, local, chips) for p in spots]

    def work(hid):
        left = jnp.concatenate(whole_pieces(piece_refs, (steps * tokens, local)), axis=1)
        total = nt(left, jnp.concatenate([down[hid, here] for here in blocks], axis=1))
        if not first:
            total = total + acc[:, hid]
        if not last:
            refs[0][:, hid] = total
            return
        threshold, _ = levels(threshold_ref, width_ref, hid)
        parts = step_rows(steps, tokens)
        grads = spikes_back([slope[r, hid] for r in parts], [total[r] for r in parts], threshold)
        grad = jnp.concatenate(grads, axis=0)
        refs[0][:, hid] = (grad * to_gate[:, hid]).astype(bf16)
        refs[1][:, hid] = (grad * to_up[:, hid]).astype(bf16)

    over_tiles(down.shape[0], 512, work)


def slopes_kernel(steps, tokens, gate, up, threshold_ref, width_ref, slope, to_gate, to_up):
    def work(hid):
        threshold, scale = levels(threshold_ref, width_ref, hid)
        gate_in, up_in = gate[:, hid], up[:, hid]
        sig = sigmoid(gate_in)
        act = gate_in * sig
        hidden = act * up_in
        parts = step_rows(steps, tokens)
        out = spikes_of([hidden[r] for r in parts], threshold, scale)
        slope[:, hid] = jnp.concatenate(slopes_of(out, scale), axis=0)
        to_gate[:, hid] = up_in * (sig * (1.0 + gate_in * (1.0 - sig)))
        to_up[:, hid] = act

    over_tiles(gate.shape[1], 256, work)


def input_grad_kernel(chips, spots, gate_grad, up_grad, gate_w, up_w, *outs):
    left = jnp.concatenate([gate_grad[...], up_grad[...]], axis=1)
    for p, out in zip(spots, outs):
        here = block_of(p, out.shape[1], chips)
        right = jnp.concatenate([gate_w[here, :], up_w[here, :]], axis=1)
        out[...] = nt(left, right).astype(out.dtype)


def per_device(
    devices,
    layer_input,
    gate_weight,
    up_weight,
    down_weight,
    hidden_threshold,
    hidden_width,
    out_threshold,
    out_width,
    out_cotangent,
):
    local = layer_input.shape[1]
    steps = layer_input.shape[2]
    tokens = layer_input.shape[3]
    rows = steps * tokens
    half = rows // 2
    hid = gate_weight.shape[2]
    chips = devices // 2
    far = chips // 2
    side = chips // 2

    order = [2 * p if p < side else 2 * (chips - 1 - p) + 1 for p in range(chips)]
    forward, backward, sibling = [], [], []
    for p in range(chips):
        a, b = order[p], order[(p + 1) % chips]
        for core in range(2):
            forward.append((2 * a + core, 2 * b + core))
            backward.append((2 * b + core, 2 * a + core))
            sibling.append((2 * a + core, 2 * a + 1 - core))
    send_fw = lambda v: lax.ppermute(v, "dp", forward)
    send_bw = lambda v: lax.ppermute(v, "dp", backward)
    swap = lambda v: lax.ppermute(v, "dp", sibling)

    x = turned(layer_input[0])
    cot = turned(out_cotangent[0])

    gate_hbm, up_hbm, down_hbm = gate_weight[0], up_weight[0], down_weight[0]
    spots = lambda at: [(d % chips) * 2 + s for d, s in at]

    def gathered(mine, take, beside):
        held, own, sib = None, [], []
        fw = bw = mine

        def taken(new, last=False):
            pieces = [p for v, _ in new for p in (v if isinstance(v, tuple) else (v,))]
            return take(pieces, [at for _, at in new], held, last)

        def swapped(new):
            return [
                (tuple(map(swap, v)) if isinstance(v, tuple) else swap(v), (d, True)) for v, (d, _) in new
            ]

        for k in range(1, far + 1):
            sent = (fw[:half], bw[half:]) if k == far else (fw, bw)
            next_fw, next_bw = send_fw(sent[0]), send_bw(sent[1])
            if k == 1:
                own = [(mine, (0, False))]
                sib = own + swapped(own)
            else:
                own = [(fw, (1 - k, False)), (bw, (k - 1, False))]
                held, sib = taken(own + sib), swapped(own)
            fw, bw = next_fw, next_bw
            fw, held, _ = lax.optimization_barrier((fw, held, beside.get(k)))
            bw = tied(bw, held)
        own = [((fw, bw), (-far, False))]
        last = swapped(own)
        held = taken(own + sib)
        return taken(last, last=True)

    def scattered(blocks_of, parts):
        def group(k):
            return [(d, s) for s in (False, True) for d in ([k, -k] if k else [0])]

        def sums(own, sib):
            return [o + s.astype(f32) for o, s in zip(own, sib)]

        sib = swap(blocks_of([(far, True)], None)[0])
        first = blocks_of([(far, False)] + group(far - 1)[2:], None)
        total = first[0] + sib.astype(f32)
        fw, bw = total[:half].astype(bf16), total[half:].astype(bf16)
        now_own, now_sib = None, first[1:]
        cut = [slice(p * rows // parts, (p + 1) * rows // parts) for p in range(parts)]
        for k in range(1, far):
            after = fw, bw
            fw, bw = send_fw(fw), send_bw(bw)
            now_sib = [swap(v) for v in now_sib]
            if k == 1:
                now_own = blocks_of(group(far - 1)[:2], after)
                fw, now_own = lax.optimization_barrier((fw, now_own))
            later = blocks_of(group(far - k - 1), after)
            fw, later = lax.optimization_barrier((fw, later))
            bw = tied(bw, later)
            a, b = sums(now_own, now_sib)
            if k == 1:
                fw = jnp.concatenate([a[:half] + fw.astype(f32), a[half:]], axis=0).astype(bf16)
                bw = jnp.concatenate([b[:half], b[half:] + bw.astype(f32)], axis=0).astype(bf16)
            else:
                fw, bw = (a + fw.astype(f32)).astype(bf16), (b + bw.astype(f32)).astype(bf16)
            now_own, now_sib = later[: len(later) // 2], later[len(later) // 2 :]
        ends = [(send_fw(fw[c]), send_bw(bw[c])) for c in cut]
        return now_own[0], swap(now_sib[0]), [e[0] for e in ends], [e[1] for e in ends], cut

    hid_level, hid_spread = hidden_threshold, hidden_width
    gate_w, up_w = call(None, [], fetch=(tied(gate_hbm, x), up_hbm))[1]
    down_w = None

    def take_inputs(pieces, at, acc, last):
        nonlocal down_w
        first = acc is None
        args = [*pieces, gate_w, up_w]
        aliases = {}
        if not first:
            aliases = {len(args): 0, len(args) + 1: 1}
            args += list(acc)
        outs = [((rows, hid), f32)] * 2
        if last:
            args += [hid_level, hid_spread]
            outs = outs + [((rows, hid), bf16)]
        res, new = call(
            functools.partial(gate_up_kernel, chips, spots(at), len(pieces), first, last, steps, tokens),
            outs,
            *args,
            flops=0,
            aliases=aliases,
            fetch=(down_hbm,) if first else (),
        )
        if new:
            down_w = new[0]
        return res

    gate, upward, spikes = gathered(x, take_inputs, {1: (gate_w, up_w)})

    def blocks(kernel, flops, *args):
        def blocks_of(at, after):
            outs = [((rows, local), bf16 if s else f32) for _, s in at]
            first = args[0] if after is None else tied(args[0], after)
            return call(functools.partial(kernel, chips, spots(at)), outs, first, *args[1:], flops=len(at) * flops)[0]

        return blocks_of

    own, sib, fw, bw, _ = scattered(blocks(down_kernel, 2 * rows * hid * local, spikes, down_w), 1)
    (emitted, current_grad, grad16), _ = call(
        functools.partial(out_kernel, steps, tokens),
        [((rows, local), bf16), ((rows, local), f32), ((rows, local), bf16)],
        own, sib, fw[0], bw[0], x, cot, out_threshold, out_width,
    )

    sections = lax.axis_size("section")
    incoming = lax.ppermute(emitted, "section", [(s, s + 1) for s in range(sections - 1)])
    way_back, _ = call(
        functools.partial(slopes_kernel, steps, tokens),
        [((rows, hid), f32)] * 3,
        tied(gate, grad16), upward, hid_level, hid_spread,
        flops=2 * rows * hid * local,
    )

    def take_grads(pieces, at, acc, last):
        first = acc is None
        args = [*pieces, down_w]
        aliases = {}
        if not first:
            if not last:
                aliases = {len(args): 0}
            args += acc
        outs = [((rows, hid), f32)]
        if last:
            args += [*way_back, hid_level, hid_spread]
            outs = [((rows, hid), bf16)] * 2
        return call(
            functools.partial(spike_grad_kernel, chips, spots(at), len(pieces), first, last, steps, tokens),
            outs,
            *args,
            flops=2 * rows * hid * local * len(at),
            aliases=aliases,
        )[0]

    gate_grad, up_grad = gathered(grad16, take_grads, {1: way_back})

    own, sib, fw, bw, cut = scattered(
        blocks(input_grad_kernel, 4 * rows * hid * local, gate_grad, up_grad, gate_w, up_w), 1
    )
    returned = []
    for c, from_fw, from_bw in zip(cut, fw, bw):
        total = own[c] + sib[c].astype(f32) + current_grad[c] + from_fw.astype(f32) + from_bw.astype(f32)
        returned.append(
            lax.ppermute(total.astype(bf16), "section", [(s + 1, s) for s in range(sections - 1)])
        )

    def viewed(v):
        return jnp.transpose(v.reshape(steps, tokens, local), (2, 0, 1))[None]

    return viewed(incoming), viewed(jnp.concatenate(returned, axis=0))


def solution(mesh):
    placed = (
        P("section", "dp", None, None),
        P("section", None, "dp"),
        P("section", None, "dp"),
        P("section", "dp", None),
        P("section", "dp"),
        P("section", "dp"),
        P("section", "dp"),
        P("section", "dp"),
        P("section", "dp", None, None),
    )
    return jax.shard_map(
        functools.partial(per_device, mesh.shape["dp"]),
        mesh=mesh,
        in_specs=placed,
        out_specs=(P("section", "dp", None, None), P("section", "dp", None, None)),
        check_vma=False,
    )
```

```python
import functools

import jax
import jax.numpy as jnp
from jax import lax
from jax.experimental import pallas as pl
from jax.experimental.pallas import tpu as pltpu
from jax.sharding import PartitionSpec as P

decay_rate = 0.9
level_unit = 0.125
f32 = jnp.float32
bf16 = jnp.bfloat16
VMEM_LIMIT = 8 * 1024 * 1024


def in_vmem(x):
    return pltpu.with_memory_space_constraint(x, pltpu.VMEM)


def call(kernel, outs, *args, flops=0, aliases=None, fetch=()):
    specs = []
    given = []
    for a in args:
        if a.dtype == jnp.int32 and a.ndim == 1:
            specs.append(pl.BlockSpec(memory_space=pltpu.SMEM))
            given.append(a)
        else:
            specs.append(pl.BlockSpec(memory_space=pltpu.VMEM))
            given.append(in_vmem(a))
    n_in, n_out, n_fetch = len(args), len(outs), len(fetch)
    specs += [pl.BlockSpec(memory_space=pltpu.HBM)] * n_fetch
    given += [pltpu.with_memory_space_constraint(w, pltpu.HBM) for w in fetch]
    outs = list(outs) + [(w.shape, w.dtype) for w in fetch]

    def body(*refs):
        ins, sources, refs = refs[:n_in], refs[n_in : n_in + n_fetch], refs[n_in + n_fetch :]
        copies = [
            pltpu.make_async_copy(sources[w], refs[n_out + w], refs[n_out + n_fetch].at[w])
            for w in range(n_fetch)
        ]
        for copy in copies:
            copy.start()
        if kernel is not None:
            kernel(*ins, *refs[:n_out])
        for copy in copies:
            copy.wait()

    res = pl.pallas_call(
        body,
        out_shape=[pltpu.VMEM(shape, dtype) for shape, dtype in outs],
        in_specs=specs,
        out_specs=[pl.BlockSpec(memory_space=pltpu.VMEM)] * len(outs),
        scratch_shapes=[pltpu.SemaphoreType.DMA((n_fetch,))] if n_fetch else [],
        input_output_aliases=aliases or {},
        compiler_params=pltpu.CompilerParams(vmem_limit_bytes=VMEM_LIMIT),
        cost_estimate=pl.CostEstimate(flops=max(flops, 1), bytes_accessed=max(flops // 512, 1), transcendentals=0),
    )(*given)
    return list(res[:n_out]), list(res[n_out:])


def nn(left, right):
    return lax.dot_general(left, right, (((1,), (0,)), ((), ())), preferred_element_type=f32)


def nt(left, right):
    return lax.dot_general(left, right, (((1,), (1,)), ((), ())), preferred_element_type=f32)


def over_tiles(total, width, work):
    width = min(width, total)

    def body(k, carry):
        work(pl.ds(pl.multiple_of(k * width, width), width))
        return carry

    lax.fori_loop(0, total // width, body, 0)


def levels(threshold_ref, width_ref, at):
    threshold = level_unit * threshold_ref[:, at].astype(f32)
    scale = 1.0 / (level_unit * width_ref[:, at].astype(f32))
    return threshold, scale


def sigmoid(v):
    return 0.5 * jnp.tanh(0.5 * v) + 0.5


def spikes_of(currents, threshold, scale):
    potential = None
    out = []
    for current in currents:
        if potential is None:
            potential = current
        else:
            potential = decay_rate * (potential - threshold * out[-1]) + current
        out.append(sigmoid((potential - threshold) * scale))
    return out


def slopes_of(spikes, scale):
    return [v * (1.0 - v) * scale for v in spikes]


def spikes_back(slopes, cotangents, threshold):
    after = None
    grads = [None] * len(slopes)
    for t in reversed(range(len(slopes))):
        if after is None:
            after = cotangents[t] * slopes[t]
        else:
            after = (cotangents[t] - decay_rate * threshold * after) * slopes[t] + decay_rate * after
        grads[t] = after
    return grads


def tied(value, after):
    return lax.optimization_barrier((value, after))[0]


def step_rows(count, tokens):
    return [slice(t * tokens, (t + 1) * tokens) for t in range(count)]


def whole_pieces(refs, shape):
    out = []
    pending = None
    for ref in refs:
        if ref.shape == shape:
            out.append(ref[...])
        elif pending is None:
            pending = ref[...]
        else:
            out.append(jnp.concatenate([pending, ref[...]], axis=0))
            pending = None
    return out


def block_of(spot, local, chips):
    index = lax.axis_index("dp")
    chip, core = index // 2, index % 2
    side = chips // 2
    place = jnp.where(chip % 2 == 0, chip // 2, chips - 1 - chip // 2)
    place = (place + spot // 2) % chips
    chip = jnp.where(place < side, 2 * place, 2 * (chips - 1 - place) + 1)
    core = 1 - core if spot % 2 else core
    return pl.ds(pl.multiple_of((2 * chip + core) * local, local), local)


def turn_kernel(raw, out):
    tokens = raw.shape[2]
    for t in range(raw.shape[1]):
        out[t * tokens : (t + 1) * tokens, :] = raw[:, t, :].astype(f32).T.astype(out.dtype)


def turned(raw):
    shape = (raw.shape[1] * raw.shape[2], raw.shape[0])
    return call(turn_kernel, [(shape, raw.dtype)], raw)[0][0]


def gate_up_kernel(chips, spots, n_pieces, first, last, steps, tokens, *refs):
    refs = list(refs)
    piece_refs, refs = refs[:n_pieces], refs[n_pieces:]
    weights, refs = refs[:2], refs[2:]
    if not first:
        acc, refs = refs[:2], refs[2:]
    if last:
        threshold_ref, width_ref = refs[:2]
        refs = refs[2:]
    local = piece_refs[0].shape[1]
    blocks = [block_of(p, local, chips) for p in spots]

    def work(cols):
        left = jnp.concatenate(whole_pieces(piece_refs, (steps * tokens, local)), axis=1)
        both = []
        for which in range(2):
            right = jnp.concatenate([weights[which][here, cols] for here in blocks], axis=0)
            total = nn(left, right)
            if not first:
                total = total + acc[which][:, cols]
            both.append(total)
            refs[which][:, cols] = total
        if last:
            threshold, scale = levels(threshold_ref, width_ref, cols)
            hidden = both[0] * sigmoid(both[0]) * both[1]
            parts = [hidden[r] for r in step_rows(steps, tokens)]
            out = spikes_of(parts, threshold, scale)
            refs[2][:, cols] = jnp.concatenate(out, axis=0).astype(bf16)

    over_tiles(refs[0].shape[1], 512, work)


def down_kernel(chips, spots, spikes, down, *outs):
    left = spikes[...]
    for p, out in zip(spots, outs):
        out[...] = nn(left, down[:, block_of(p, out.shape[1], chips)]).astype(out.dtype)


def out_kernel(steps, tokens, own, sib, fw, bw, x, cot, threshold_ref, width_ref, emitted, grad, grad16):
    threshold, scale = levels(threshold_ref, width_ref, slice(None))
    current = (
        own[...] + sib[...].astype(f32) + fw[...].astype(f32) + bw[...].astype(f32) + x[...].astype(f32)
    )
    rows = step_rows(steps, tokens)
    out = spikes_of([current[r] for r in rows], threshold, scale)
    emitted[...] = jnp.concatenate(out, axis=0).astype(bf16)
    grads = spikes_back(slopes_of(out, scale), [cot[r, :].astype(f32) for r in rows], threshold)
    total = jnp.concatenate(grads, axis=0)
    grad[...] = total
    grad16[...] = total.astype(bf16)


def spike_grad_kernel(chips, spots, n_pieces, first, last, steps, tokens, *refs):
    refs = list(refs)
    piece_refs, refs = refs[:n_pieces], refs[n_pieces:]
    down, refs = refs[0], refs[1:]
    if not first:
        acc, refs = refs[0], refs[1:]
    if last:
        slope, to_gate, to_up, threshold_ref, width_ref = refs[:5]
        refs = refs[5:]
    local = piece_refs[0].shape[1]
    blocks = [block_of(p, local, chips) for p in spots]

    def work(hid):
        left = jnp.concatenate(whole_pieces(piece_refs, (steps * tokens, local)), axis=1)
        total = nt(left, jnp.concatenate([down[hid, here] for here in blocks], axis=1))
        if not first:
            total = total + acc[:, hid]
        if not last:
            refs[0][:, hid] = total
            return
        threshold, _ = levels(threshold_ref, width_ref, hid)
        parts = step_rows(steps, tokens)
        grads = spikes_back([slope[r, hid] for r in parts], [total[r] for r in parts], threshold)
        grad = jnp.concatenate(grads, axis=0)
        refs[0][:, hid] = (grad * to_gate[:, hid]).astype(bf16)
        refs[1][:, hid] = (grad * to_up[:, hid]).astype(bf16)

    over_tiles(down.shape[0], 512, work)


def slopes_kernel(steps, tokens, gate, up, threshold_ref, width_ref, slope, to_gate, to_up):
    def work(hid):
        threshold, scale = levels(threshold_ref, width_ref, hid)
        gate_in, up_in = gate[:, hid], up[:, hid]
        sig = sigmoid(gate_in)
        act = gate_in * sig
        hidden = act * up_in
        parts = step_rows(steps, tokens)
        out = spikes_of([hidden[r] for r in parts], threshold, scale)
        slope[:, hid] = jnp.concatenate(slopes_of(out, scale), axis=0)
        to_gate[:, hid] = up_in * (sig * (1.0 + gate_in * (1.0 - sig)))
        to_up[:, hid] = act

    over_tiles(gate.shape[1], 256, work)


def input_grad_kernel(chips, spots, gate_grad, up_grad, gate_w, up_w, *outs):
    left = jnp.concatenate([gate_grad[...], up_grad[...]], axis=1)
    for p, out in zip(spots, outs):
        here = block_of(p, out.shape[1], chips)
        right = jnp.concatenate([gate_w[here, :], up_w[here, :]], axis=1)
        out[...] = nt(left, right).astype(out.dtype)


def per_device(
    devices,
    layer_input,
    gate_weight,
    up_weight,
    down_weight,
    hidden_threshold,
    hidden_width,
    out_threshold,
    out_width,
    out_cotangent,
):
    local = layer_input.shape[1]
    steps = layer_input.shape[2]
    tokens = layer_input.shape[3]
    rows = steps * tokens
    half = rows // 2
    hid = gate_weight.shape[2]
    chips = devices // 2
    far = chips // 2
    side = chips // 2

    order = [2 * p if p < side else 2 * (chips - 1 - p) + 1 for p in range(chips)]
    forward, backward, sibling = [], [], []
    for p in range(chips):
        a, b = order[p], order[(p + 1) % chips]
        for core in range(2):
            forward.append((2 * a + core, 2 * b + core))
            backward.append((2 * b + core, 2 * a + core))
            sibling.append((2 * a + core, 2 * a + 1 - core))
    send_fw = lambda v: lax.ppermute(v, "dp", forward)
    send_bw = lambda v: lax.ppermute(v, "dp", backward)
    swap = lambda v: lax.ppermute(v, "dp", sibling)

    x = turned(layer_input[0])
    cot = turned(out_cotangent[0])

    gate_hbm, up_hbm, down_hbm = gate_weight[0], up_weight[0], down_weight[0]
    spots = lambda at: [(d % chips) * 2 + s for d, s in at]

    def gathered(mine, take, beside, early):
        held, own, sib = None, [], []
        fw = bw = mine

        def taken(new, last=False):
            pieces = [p for v, _ in new for p in (v if isinstance(v, tuple) else (v,))]
            return take(pieces, [at for _, at in new], held, last)

        def swapped(new):
            return [
                (tuple(map(swap, v)) if isinstance(v, tuple) else swap(v), (d, True)) for v, (d, _) in new
            ]

        for k in range(1, far + 1):
            sent = (fw[:half], bw[half:]) if k == far else (fw, bw)
            next_fw, next_bw = send_fw(sent[0]), send_bw(sent[1])
            if k == 1:
                own = [(mine, (0, False))]
                sib = own + swapped(own)
            else:
                own = [(fw, (1 - k, False)), (bw, (k - 1, False))]
                held, sib = taken(own + sib), swapped(own)
                if k == far and early:
                    held, sib = taken(sib), []
            fw, bw = next_fw, next_bw
            fw, held, _ = lax.optimization_barrier((fw, held, beside.get(k)))
            bw = tied(bw, held)
        own = [((fw, bw), (-far, False))]
        last = swapped(own)
        held = taken(own + sib)
        return taken(last, last=True)

    def scattered(blocks_of, parts):
        def group(k):
            return [(d, s) for s in (False, True) for d in ([k, -k] if k else [0])]

        def sums(own, sib):
            return [o + s.astype(f32) for o, s in zip(own, sib)]

        sib = swap(blocks_of([(far, True)], None)[0])
        first = blocks_of([(far, False)] + group(far - 1)[2:], None)
        total = first[0] + sib.astype(f32)
        fw, bw = total[:half].astype(bf16), total[half:].astype(bf16)
        now_own, now_sib = None, first[1:]
        cut = [slice(p * rows // parts, (p + 1) * rows // parts) for p in range(parts)]
        for k in range(1, far):
            after = fw, bw
            fw, bw = send_fw(fw), send_bw(bw)
            now_sib = [swap(v) for v in now_sib]
            if k == 1:
                now_own = blocks_of(group(far - 1)[:2], after)
                fw, now_own = lax.optimization_barrier((fw, now_own))
            later = blocks_of(group(far - k - 1), after)
            fw, later = lax.optimization_barrier((fw, later))
            bw = tied(bw, later)
            a, b = sums(now_own, now_sib)
            if k == 1:
                fw = jnp.concatenate([a[:half] + fw.astype(f32), a[half:]], axis=0).astype(bf16)
                bw = jnp.concatenate([b[:half], b[half:] + tied(bw, fw).astype(f32)], axis=0).astype(bf16)
            else:
                fw = (a + fw.astype(f32)).astype(bf16)
                bw = (b + tied(bw, fw).astype(f32)).astype(bf16)
            now_own, now_sib = later[: len(later) // 2], later[len(later) // 2 :]
        ends = [(send_fw(fw[c]), send_bw(bw[c])) for c in cut]
        return now_own[0], swap(now_sib[0]), [e[0] for e in ends], [e[1] for e in ends], cut

    hid_level, hid_spread = hidden_threshold, hidden_width
    gate_w, up_w = call(None, [], fetch=(tied(gate_hbm, x), up_hbm))[1]
    down_w = None

    def take_inputs(pieces, at, acc, last):
        nonlocal down_w
        first = acc is None
        args = [*pieces, gate_w, up_w]
        aliases = {}
        if not first:
            aliases = {len(args): 0, len(args) + 1: 1}
            args += list(acc)
        outs = [((rows, hid), f32)] * 2
        if last:
            args += [hid_level, hid_spread]
            outs = outs + [((rows, hid), bf16)]
        res, new = call(
            functools.partial(gate_up_kernel, chips, spots(at), len(pieces), first, last, steps, tokens),
            outs,
            *args,
            flops=0,
            aliases=aliases,
            fetch=(down_hbm,) if first else (),
        )
        if new:
            down_w = new[0]
        return res

    gate, upward, spikes = gathered(x, take_inputs, {1: (gate_w, up_w)}, False)

    def blocks(kernel, flops, *args):
        def blocks_of(at, after):
            outs = [((rows, local), bf16 if s else f32) for _, s in at]
            first = args[0] if after is None else tied(args[0], after)
            return call(functools.partial(kernel, chips, spots(at)), outs, first, *args[1:], flops=len(at) * flops)[0]

        return blocks_of

    own, sib, fw, bw, _ = scattered(blocks(down_kernel, 2 * rows * hid * local, spikes, down_w), 1)
    (emitted, current_grad, grad16), _ = call(
        functools.partial(out_kernel, steps, tokens),
        [((rows, local), bf16), ((rows, local), f32), ((rows, local), bf16)],
        own, sib, fw[0], bw[0], x, cot, out_threshold, out_width,
    )

    sections = lax.axis_size("section")
    incoming = lax.ppermute(emitted, "section", [(s, s + 1) for s in range(sections - 1)])
    way_back, _ = call(
        functools.partial(slopes_kernel, steps, tokens),
        [((rows, hid), f32)] * 3,
        tied(gate, grad16), upward, hid_level, hid_spread,
        flops=2 * rows * hid * local,
    )

    def take_grads(pieces, at, acc, last):
        first = acc is None
        args = [*pieces, down_w]
        aliases = {}
        if not first:
            if not last:
                aliases = {len(args): 0}
            args += acc
        outs = [((rows, hid), f32)]
        if last:
            args += [*way_back, hid_level, hid_spread]
            outs = [((rows, hid), bf16)] * 2
        return call(
            functools.partial(spike_grad_kernel, chips, spots(at), len(pieces), first, last, steps, tokens),
            outs,
            *args,
            flops=2 * rows * hid * local * len(at),
            aliases=aliases,
        )[0]

    gate_grad, up_grad = gathered(grad16, take_grads, {1: way_back}, True)

    own, sib, fw, bw, cut = scattered(
        blocks(input_grad_kernel, 4 * rows * hid * local, gate_grad, up_grad, gate_w, up_w), 1
    )
    returned = []
    for c, from_fw, from_bw in zip(cut, fw, bw):
        total = own[c] + sib[c].astype(f32) + current_grad[c] + from_fw.astype(f32) + from_bw.astype(f32)
        returned.append(
            lax.ppermute(total.astype(bf16), "section", [(s + 1, s) for s in range(sections - 1)])
        )

    def viewed(v):
        return jnp.transpose(v.reshape(steps, tokens, local), (2, 0, 1))[None]

    return viewed(incoming), viewed(jnp.concatenate(returned, axis=0))


def solution(mesh):
    placed = (
        P("section", "dp", None, None),
        P("section", None, "dp"),
        P("section", None, "dp"),
        P("section", "dp", None),
        P("section", "dp"),
        P("section", "dp"),
        P("section", "dp"),
        P("section", "dp"),
        P("section", "dp", None, None),
    )
    return jax.shard_map(
        functools.partial(per_device, mesh.shape["dp"]),
        mesh=mesh,
        in_specs=placed,
        out_specs=(P("section", "dp", None, None), P("section", "dp", None, None)),
        check_vma=False,
    )
```

```python
import functools

import jax
import jax.numpy as jnp
from jax import lax
from jax.experimental import pallas as pl
from jax.experimental.pallas import tpu as pltpu
from jax.sharding import PartitionSpec as P

decay_rate = 0.9
level_unit = 0.125
f32 = jnp.float32
bf16 = jnp.bfloat16
VMEM_LIMIT = 8 * 1024 * 1024


def in_vmem(x):
    return pltpu.with_memory_space_constraint(x, pltpu.VMEM)


def call(kernel, outs, *args, flops=0, aliases=None, fetch=()):
    specs = []
    given = []
    for a in args:
        if a.dtype == jnp.int32 and a.ndim == 1:
            specs.append(pl.BlockSpec(memory_space=pltpu.SMEM))
            given.append(a)
        else:
            specs.append(pl.BlockSpec(memory_space=pltpu.VMEM))
            given.append(in_vmem(a))
    n_in, n_out, n_fetch = len(args), len(outs), len(fetch)
    specs += [pl.BlockSpec(memory_space=pltpu.HBM)] * n_fetch
    given += [pltpu.with_memory_space_constraint(w, pltpu.HBM) for w in fetch]
    outs = list(outs) + [(w.shape, w.dtype) for w in fetch]

    def body(*refs):
        ins, sources, refs = refs[:n_in], refs[n_in : n_in + n_fetch], refs[n_in + n_fetch :]
        copies = [
            pltpu.make_async_copy(sources[w], refs[n_out + w], refs[n_out + n_fetch].at[w])
            for w in range(n_fetch)
        ]
        for copy in copies:
            copy.start()
        if kernel is not None:
            kernel(*ins, *refs[:n_out])
        for copy in copies:
            copy.wait()

    res = pl.pallas_call(
        body,
        out_shape=[pltpu.VMEM(shape, dtype) for shape, dtype in outs],
        in_specs=specs,
        out_specs=[pl.BlockSpec(memory_space=pltpu.VMEM)] * len(outs),
        scratch_shapes=[pltpu.SemaphoreType.DMA((n_fetch,))] if n_fetch else [],
        input_output_aliases=aliases or {},
        compiler_params=pltpu.CompilerParams(vmem_limit_bytes=VMEM_LIMIT),
        cost_estimate=pl.CostEstimate(flops=max(flops, 1), bytes_accessed=max(flops // 512, 1), transcendentals=0),
    )(*given)
    return list(res[:n_out]), list(res[n_out:])


def nn(left, right):
    return lax.dot_general(left, right, (((1,), (0,)), ((), ())), preferred_element_type=f32)


def nt(left, right):
    return lax.dot_general(left, right, (((1,), (1,)), ((), ())), preferred_element_type=f32)


def over_tiles(total, width, work):
    width = min(width, total)

    def body(k, carry):
        work(pl.ds(pl.multiple_of(k * width, width), width))
        return carry

    lax.fori_loop(0, total // width, body, 0)


def levels(threshold_ref, width_ref, at):
    threshold = level_unit * threshold_ref[:, at].astype(f32)
    scale = 1.0 / (level_unit * width_ref[:, at].astype(f32))
    return threshold, scale


def sigmoid(v):
    return 0.5 * jnp.tanh(0.5 * v) + 0.5


def spikes_of(currents, threshold, scale):
    potential = None
    out = []
    for current in currents:
        if potential is None:
            potential = current
        else:
            potential = decay_rate * (potential - threshold * out[-1]) + current
        out.append(sigmoid((potential - threshold) * scale))
    return out


def slopes_of(spikes, scale):
    return [v * (1.0 - v) * scale for v in spikes]


def spikes_back(slopes, cotangents, threshold):
    after = None
    grads = [None] * len(slopes)
    for t in reversed(range(len(slopes))):
        if after is None:
            after = cotangents[t] * slopes[t]
        else:
            after = (cotangents[t] - decay_rate * threshold * after) * slopes[t] + decay_rate * after
        grads[t] = after
    return grads


def tied(value, after):
    return lax.optimization_barrier((value, after))[0]


def step_rows(count, tokens):
    return [slice(t * tokens, (t + 1) * tokens) for t in range(count)]


def whole_pieces(refs, shape):
    out = []
    pending = None
    for ref in refs:
        if ref.shape == shape:
            out.append(ref[...])
        elif pending is None:
            pending = ref[...]
        else:
            out.append(jnp.concatenate([pending, ref[...]], axis=0))
            pending = None
    return out


def block_of(spot, local, chips):
    index = lax.axis_index("dp")
    chip, core = index // 2, index % 2
    side = chips // 2
    place = jnp.where(chip % 2 == 0, chip // 2, chips - 1 - chip // 2)
    place = (place + spot // 2) % chips
    chip = jnp.where(place < side, 2 * place, 2 * (chips - 1 - place) + 1)
    core = 1 - core if spot % 2 else core
    return pl.ds(pl.multiple_of((2 * chip + core) * local, local), local)


def turn_kernel(raw, out):
    tokens = raw.shape[2]
    whole = raw[...].astype(f32)
    for t in range(raw.shape[1]):
        out[t * tokens : (t + 1) * tokens, :] = whole[:, t, :].T.astype(out.dtype)


def turned(raw):
    shape = (raw.shape[1] * raw.shape[2], raw.shape[0])
    return call(turn_kernel, [(shape, raw.dtype)], raw)[0][0]


def gate_up_kernel(chips, spots, n_pieces, first, last, steps, tokens, *refs):
    refs = list(refs)
    piece_refs, refs = refs[:n_pieces], refs[n_pieces:]
    weights, refs = refs[:2], refs[2:]
    if not first:
        acc, refs = refs[:2], refs[2:]
    if last:
        threshold_ref, width_ref = refs[:2]
        refs = refs[2:]
    local = piece_refs[0].shape[1]
    blocks = [block_of(p, local, chips) for p in spots]

    def work(cols):
        left = jnp.concatenate(whole_pieces(piece_refs, (steps * tokens, local)), axis=1)
        both = []
        for which in range(2):
            right = jnp.concatenate([weights[which][here, cols] for here in blocks], axis=0)
            total = nn(left, right)
            if not first:
                total = total + acc[which][:, cols]
            both.append(total)
            refs[which][:, cols] = total
        if last:
            threshold, scale = levels(threshold_ref, width_ref, cols)
            hidden = both[0] * sigmoid(both[0]) * both[1]
            parts = [hidden[r] for r in step_rows(steps, tokens)]
            out = spikes_of(parts, threshold, scale)
            refs[2][:, cols] = jnp.concatenate(out, axis=0).astype(bf16)

    over_tiles(refs[0].shape[1], 512, work)


def down_kernel(chips, spots, spikes, down, *outs):
    left = spikes[...]
    for p, out in zip(spots, outs):
        out[...] = nn(left, down[:, block_of(p, out.shape[1], chips)]).astype(out.dtype)


def out_kernel(steps, tokens, own, sib, fw, bw, x, cot, threshold_ref, width_ref, emitted, grad, grad16):
    threshold, scale = levels(threshold_ref, width_ref, slice(None))
    current = (
        own[...] + sib[...].astype(f32) + fw[...].astype(f32) + bw[...].astype(f32) + x[...].astype(f32)
    )
    rows = step_rows(steps, tokens)
    out = spikes_of([current[r] for r in rows], threshold, scale)
    emitted[...] = jnp.concatenate(out, axis=0).astype(bf16)
    grads = spikes_back(slopes_of(out, scale), [cot[r, :].astype(f32) for r in rows], threshold)
    total = jnp.concatenate(grads, axis=0)
    grad[...] = total
    grad16[...] = total.astype(bf16)


def spike_grad_kernel(chips, spots, n_pieces, first, last, steps, tokens, *refs):
    refs = list(refs)
    piece_refs, refs = refs[:n_pieces], refs[n_pieces:]
    down, refs = refs[0], refs[1:]
    if not first:
        acc, refs = refs[0], refs[1:]
    if last:
        slope, to_gate, to_up, threshold_ref, width_ref = refs[:5]
        refs = refs[5:]
    local = piece_refs[0].shape[1]
    blocks = [block_of(p, local, chips) for p in spots]

    def work(hid):
        left = jnp.concatenate(whole_pieces(piece_refs, (steps * tokens, local)), axis=1)
        total = nt(left, jnp.concatenate([down[hid, here] for here in blocks], axis=1))
        if not first:
            total = total + acc[:, hid]
        if not last:
            refs[0][:, hid] = total
            return
        threshold, _ = levels(threshold_ref, width_ref, hid)
        parts = step_rows(steps, tokens)
        grads = spikes_back([slope[r, hid] for r in parts], [total[r] for r in parts], threshold)
        grad = jnp.concatenate(grads, axis=0)
        refs[0][:, hid] = (grad * to_gate[:, hid]).astype(bf16)
        refs[1][:, hid] = (grad * to_up[:, hid]).astype(bf16)

    over_tiles(down.shape[0], 512, work)


def slopes_kernel(steps, tokens, gate, up, threshold_ref, width_ref, slope, to_gate, to_up):
    def work(hid):
        threshold, scale = levels(threshold_ref, width_ref, hid)
        gate_in, up_in = gate[:, hid], up[:, hid]
        sig = sigmoid(gate_in)
        act = gate_in * sig
        hidden = act * up_in
        parts = step_rows(steps, tokens)
        out = spikes_of([hidden[r] for r in parts], threshold, scale)
        slope[:, hid] = jnp.concatenate(slopes_of(out, scale), axis=0)
        to_gate[:, hid] = up_in * (sig * (1.0 + gate_in * (1.0 - sig)))
        to_up[:, hid] = act

    over_tiles(gate.shape[1], 256, work)


def input_grad_kernel(chips, spots, gate_grad, up_grad, gate_w, up_w, *outs):
    left = jnp.concatenate([gate_grad[...], up_grad[...]], axis=1)
    for p, out in zip(spots, outs):
        here = block_of(p, out.shape[1], chips)
        right = jnp.concatenate([gate_w[here, :], up_w[here, :]], axis=1)
        out[...] = nt(left, right).astype(out.dtype)


def per_device(
    devices,
    layer_input,
    gate_weight,
    up_weight,
    down_weight,
    hidden_threshold,
    hidden_width,
    out_threshold,
    out_width,
    out_cotangent,
):
    local = layer_input.shape[1]
    steps = layer_input.shape[2]
    tokens = layer_input.shape[3]
    rows = steps * tokens
    half = rows // 2
    hid = gate_weight.shape[2]
    chips = devices // 2
    far = chips // 2
    side = chips // 2

    order = [2 * p if p < side else 2 * (chips - 1 - p) + 1 for p in range(chips)]
    forward, backward, sibling = [], [], []
    for p in range(chips):
        a, b = order[p], order[(p + 1) % chips]
        for core in range(2):
            forward.append((2 * a + core, 2 * b + core))
            backward.append((2 * b + core, 2 * a + core))
            sibling.append((2 * a + core, 2 * a + 1 - core))
    send_fw = lambda v: lax.ppermute(v, "dp", forward)
    send_bw = lambda v: lax.ppermute(v, "dp", backward)
    swap = lambda v: lax.ppermute(v, "dp", sibling)

    x = turned(layer_input[0])
    cot = turned(out_cotangent[0])

    gate_hbm, up_hbm, down_hbm = gate_weight[0], up_weight[0], down_weight[0]
    spots = lambda at: [(d % chips) * 2 + s for d, s in at]

    def gathered(mine, take, beside, early):
        held, own, sib = None, [], []
        fw = bw = mine

        def taken(new, last=False):
            pieces = [p for v, _ in new for p in (v if isinstance(v, tuple) else (v,))]
            return take(pieces, [at for _, at in new], held, last)

        def swapped(new):
            return [
                (tuple(map(swap, v)) if isinstance(v, tuple) else swap(v), (d, True)) for v, (d, _) in new
            ]

        for k in range(1, far + 1):
            sent = (fw[:half], bw[half:]) if k == far else (fw, bw)
            if early:
                next_fw, next_bw = send_fw(sent[0]), send_bw(sent[1])
            else:
                next_bw, next_fw = send_bw(sent[1]), send_fw(sent[0])
            if k == 1:
                own = [(mine, (0, False))]
                sib = own + swapped(own)
            else:
                own = [(fw, (1 - k, False)), (bw, (k - 1, False))]
                held, sib = taken(own + sib), swapped(own)
                if k == far and early:
                    held, sib = taken(sib), []
            fw, bw = next_fw, next_bw
            bw, held, _ = lax.optimization_barrier((bw, held, beside.get(k)))
            fw = tied(fw, (held, bw) if not early else held)
            if early:
                bw = tied(bw, held)
        own = [((fw, bw), (-far, False))]
        last = swapped(own)
        held = taken(own + sib)
        return taken(last, last=True)

    def scattered(blocks_of, parts):
        def group(k):
            return [(d, s) for s in (False, True) for d in ([k, -k] if k else [0])]

        def sums(own, sib):
            return [o + s.astype(f32) for o, s in zip(own, sib)]

        sib = swap(blocks_of([(far, True)], None)[0])
        first = blocks_of([(far, False)] + group(far - 1)[2:], None)
        total = first[0] + sib.astype(f32)
        fw, bw = total[:half].astype(bf16), total[half:].astype(bf16)
        now_own, now_sib = None, first[1:]
        cut = [slice(p * rows // parts, (p + 1) * rows // parts) for p in range(parts)]
        for k in range(1, far):
            after = fw, bw
            fw, bw = send_fw(fw), send_bw(bw)
            now_sib = [swap(v) for v in now_sib]
            if k == 1:
                now_own = blocks_of(group(far - 1)[:2], after)
                fw, now_own = lax.optimization_barrier((fw, now_own))
            later = blocks_of(group(far - k - 1), after)
            fw, later = lax.optimization_barrier((fw, later))
            bw = tied(bw, later)
            a, b = sums(now_own, now_sib)
            if k == 1:
                fw = jnp.concatenate([a[:half] + fw.astype(f32), a[half:]], axis=0).astype(bf16)
                bw = jnp.concatenate([b[:half], b[half:] + tied(bw, fw).astype(f32)], axis=0).astype(bf16)
            else:
                fw = (a + fw.astype(f32)).astype(bf16)
                bw = (b + tied(bw, fw).astype(f32)).astype(bf16)
            now_own, now_sib = later[: len(later) // 2], later[len(later) // 2 :]
        ends = [(send_fw(fw[c]), send_bw(bw[c])) for c in cut]
        return now_own[0], swap(now_sib[0]), [e[0] for e in ends], [e[1] for e in ends], cut

    hid_level, hid_spread = hidden_threshold, hidden_width
    gate_w, up_w = call(None, [], fetch=(tied(gate_hbm, x), up_hbm))[1]
    down_w = None

    def take_inputs(pieces, at, acc, last):
        nonlocal down_w
        first = acc is None
        args = [*pieces, gate_w, up_w]
        aliases = {}
        if not first:
            aliases = {len(args): 0, len(args) + 1: 1}
            args += list(acc)
        outs = [((rows, hid), f32)] * 2
        if last:
            args += [hid_level, hid_spread]
            outs = outs + [((rows, hid), bf16)]
        res, new = call(
            functools.partial(gate_up_kernel, chips, spots(at), len(pieces), first, last, steps, tokens),
            outs,
            *args,
            flops=0,
            aliases=aliases,
            fetch=(down_hbm,) if first else (),
        )
        if new:
            down_w = new[0]
        return res

    gate, upward, spikes = gathered(x, take_inputs, {1: (gate_w, up_w)}, False)

    def blocks(kernel, flops, *args):
        def blocks_of(at, after):
            outs = [((rows, local), bf16 if s else f32) for _, s in at]
            first = args[0] if after is None else tied(args[0], after)
            return call(functools.partial(kernel, chips, spots(at)), outs, first, *args[1:], flops=len(at) * flops)[0]

        return blocks_of

    own, sib, fw, bw, _ = scattered(blocks(down_kernel, 2 * rows * hid * local, spikes, down_w), 1)
    (emitted, current_grad, grad16), _ = call(
        functools.partial(out_kernel, steps, tokens),
        [((rows, local), bf16), ((rows, local), f32), ((rows, local), bf16)],
        own, sib, fw[0], bw[0], x, cot, out_threshold, out_width,
    )

    sections = lax.axis_size("section")
    incoming = lax.ppermute(emitted, "section", [(s, s + 1) for s in range(sections - 1)])
    way_back, _ = call(
        functools.partial(slopes_kernel, steps, tokens),
        [((rows, hid), f32)] * 3,
        tied(gate, grad16), upward, hid_level, hid_spread,
        flops=2 * rows * hid * local,
    )

    def take_grads(pieces, at, acc, last):
        first = acc is None
        args = [*pieces, down_w]
        aliases = {}
        if not first:
            if not last:
                aliases = {len(args): 0}
            args += acc
        outs = [((rows, hid), f32)]
        if last:
            args += [*way_back, hid_level, hid_spread]
            outs = [((rows, hid), bf16)] * 2
        return call(
            functools.partial(spike_grad_kernel, chips, spots(at), len(pieces), first, last, steps, tokens),
            outs,
            *args,
            flops=2 * rows * hid * local * len(at),
            aliases=aliases,
        )[0]

    gate_grad, up_grad = gathered(grad16, take_grads, {1: way_back}, True)

    own, sib, fw, bw, cut = scattered(
        blocks(input_grad_kernel, 4 * rows * hid * local, gate_grad, up_grad, gate_w, up_w), 1
    )
    returned = []
    for c, from_fw, from_bw in zip(cut, fw, bw):
        total = own[c] + sib[c].astype(f32) + current_grad[c] + from_fw.astype(f32) + from_bw.astype(f32)
        returned.append(
            lax.ppermute(total.astype(bf16), "section", [(s + 1, s) for s in range(sections - 1)])
        )

    def viewed(v):
        return jnp.transpose(v.reshape(steps, tokens, local), (2, 0, 1))[None]

    return viewed(incoming), viewed(jnp.concatenate(returned, axis=0))


def solution(mesh):
    placed = (
        P("section", "dp", None, None),
        P("section", None, "dp"),
        P("section", None, "dp"),
        P("section", "dp", None),
        P("section", "dp"),
        P("section", "dp"),
        P("section", "dp"),
        P("section", "dp"),
        P("section", "dp", None, None),
    )
    return jax.shard_map(
        functools.partial(per_device, mesh.shape["dp"]),
        mesh=mesh,
        in_specs=placed,
        out_specs=(P("section", "dp", None, None), P("section", "dp", None, None)),
        check_vma=False,
    )
```

```python
import functools

import jax
import jax.numpy as jnp
from jax import lax
from jax.experimental import pallas as pl
from jax.experimental.pallas import tpu as pltpu
from jax.sharding import PartitionSpec as P

decay_rate = 0.9
level_unit = 0.125
f32 = jnp.float32
bf16 = jnp.bfloat16
VMEM_LIMIT = 8 * 1024 * 1024


def in_vmem(x):
    return pltpu.with_memory_space_constraint(x, pltpu.VMEM)


def call(kernel, outs, *args, flops=0, aliases=None, fetch=()):
    specs = []
    given = []
    for a in args:
        if a.dtype == jnp.int32 and a.ndim == 1:
            specs.append(pl.BlockSpec(memory_space=pltpu.SMEM))
            given.append(a)
        else:
            specs.append(pl.BlockSpec(memory_space=pltpu.VMEM))
            given.append(in_vmem(a))
    n_in, n_out, n_fetch = len(args), len(outs), len(fetch)
    specs += [pl.BlockSpec(memory_space=pltpu.HBM)] * n_fetch
    given += [pltpu.with_memory_space_constraint(w, pltpu.HBM) for w in fetch]
    outs = list(outs) + [(w.shape, w.dtype) for w in fetch]

    def body(*refs):
        ins, sources, refs = refs[:n_in], refs[n_in : n_in + n_fetch], refs[n_in + n_fetch :]
        copies = [
            pltpu.make_async_copy(sources[w], refs[n_out + w], refs[n_out + n_fetch].at[w])
            for w in range(n_fetch)
        ]
        for copy in copies:
            copy.start()
        if kernel is not None:
            kernel(*ins, *refs[:n_out])
        for copy in copies:
            copy.wait()

    res = pl.pallas_call(
        body,
        out_shape=[pltpu.VMEM(shape, dtype) for shape, dtype in outs],
        in_specs=specs,
        out_specs=[pl.BlockSpec(memory_space=pltpu.VMEM)] * len(outs),
        scratch_shapes=[pltpu.SemaphoreType.DMA((n_fetch,))] if n_fetch else [],
        input_output_aliases=aliases or {},
        compiler_params=pltpu.CompilerParams(vmem_limit_bytes=VMEM_LIMIT),
        cost_estimate=pl.CostEstimate(flops=max(flops, 1), bytes_accessed=max(flops // 512, 1), transcendentals=0),
    )(*given)
    return list(res[:n_out]), list(res[n_out:])


def nn(left, right):
    return lax.dot_general(left, right, (((1,), (0,)), ((), ())), preferred_element_type=f32)


def nt(left, right):
    return lax.dot_general(left, right, (((1,), (1,)), ((), ())), preferred_element_type=f32)


def over_tiles(total, width, work):
    width = min(width, total)

    def body(k, carry):
        work(pl.ds(pl.multiple_of(k * width, width), width))
        return carry

    lax.fori_loop(0, total // width, body, 0)


def levels(threshold_ref, width_ref, at):
    threshold = level_unit * threshold_ref[:, at].astype(f32)
    scale = 1.0 / (level_unit * width_ref[:, at].astype(f32))
    return threshold, scale


def sigmoid(v):
    return 0.5 * jnp.tanh(0.5 * v) + 0.5


def spikes_of(currents, threshold, scale):
    potential = None
    out = []
    for current in currents:
        if potential is None:
            potential = current
        else:
            potential = decay_rate * (potential - threshold * out[-1]) + current
        out.append(sigmoid((potential - threshold) * scale))
    return out


def slopes_of(spikes, scale):
    return [v * (1.0 - v) * scale for v in spikes]


def spikes_back(slopes, cotangents, threshold):
    after = None
    grads = [None] * len(slopes)
    for t in reversed(range(len(slopes))):
        if after is None:
            after = cotangents[t] * slopes[t]
        else:
            after = (cotangents[t] - decay_rate * threshold * after) * slopes[t] + decay_rate * after
        grads[t] = after
    return grads


def tied(value, after):
    return lax.optimization_barrier((value, after))[0]


def step_rows(count, tokens):
    return [slice(t * tokens, (t + 1) * tokens) for t in range(count)]


def whole_pieces(refs, shape):
    out = []
    pending = None
    for ref in refs:
        if ref.shape == shape:
            out.append(ref[...])
        elif pending is None:
            pending = ref[...]
        else:
            out.append(jnp.concatenate([pending, ref[...]], axis=0))
            pending = None
    return out


def block_of(spot, local, chips):
    index = lax.axis_index("dp")
    chip, core = index // 2, index % 2
    side = chips // 2
    place = jnp.where(chip % 2 == 0, chip // 2, chips - 1 - chip // 2)
    place = (place + spot // 2) % chips
    chip = jnp.where(place < side, 2 * place, 2 * (chips - 1 - place) + 1)
    core = 1 - core if spot % 2 else core
    return pl.ds(pl.multiple_of((2 * chip + core) * local, local), local)


def turn_kernel(raw, out):
    tokens = raw.shape[2]
    whole = raw[...].astype(f32)
    for t in range(raw.shape[1]):
        out[t * tokens : (t + 1) * tokens, :] = whole[:, t, :].T.astype(out.dtype)


def turned(raw):
    shape = (raw.shape[1] * raw.shape[2], raw.shape[0])
    return call(turn_kernel, [(shape, raw.dtype)], raw)[0][0]


def gate_up_kernel(chips, spots, n_pieces, first, last, steps, tokens, *refs):
    refs = list(refs)
    piece_refs, refs = refs[:n_pieces], refs[n_pieces:]
    weights, refs = refs[:2], refs[2:]
    if not first:
        acc, refs = refs[:2], refs[2:]
    if last:
        threshold_ref, width_ref = refs[:2]
        refs = refs[2:]
    local = piece_refs[0].shape[1]
    blocks = [block_of(p, local, chips) for p in spots]

    def work(cols):
        left = jnp.concatenate(whole_pieces(piece_refs, (steps * tokens, local)), axis=1)
        both = []
        for which in range(2):
            right = jnp.concatenate([weights[which][here, cols] for here in blocks], axis=0)
            total = nn(left, right)
            if not first:
                total = total + acc[which][:, cols]
            both.append(total)
            refs[which][:, cols] = total
        if last:
            threshold, scale = levels(threshold_ref, width_ref, cols)
            hidden = both[0] * sigmoid(both[0]) * both[1]
            parts = [hidden[r] for r in step_rows(steps, tokens)]
            out = spikes_of(parts, threshold, scale)
            refs[2][:, cols] = jnp.concatenate(out, axis=0).astype(bf16)

    over_tiles(refs[0].shape[1], 512, work)


def down_kernel(chips, spots, spikes, down, *outs):
    left = spikes[...]
    for p, out in zip(spots, outs):
        out[...] = nn(left, down[:, block_of(p, out.shape[1], chips)]).astype(out.dtype)


def out_kernel(steps, tokens, own, sib, fw, bw, x, cot, threshold_ref, width_ref, emitted, grad, grad16):
    threshold, scale = levels(threshold_ref, width_ref, slice(None))
    current = (
        own[...] + sib[...].astype(f32) + fw[...].astype(f32) + bw[...].astype(f32) + x[...].astype(f32)
    )
    rows = step_rows(steps, tokens)
    out = spikes_of([current[r] for r in rows], threshold, scale)
    emitted[...] = jnp.concatenate(out, axis=0).astype(bf16)
    grads = spikes_back(slopes_of(out, scale), [cot[r, :].astype(f32) for r in rows], threshold)
    total = jnp.concatenate(grads, axis=0)
    grad[...] = total
    grad16[...] = total.astype(bf16)


def spike_grad_kernel(chips, spots, n_pieces, first, last, steps, tokens, *refs):
    refs = list(refs)
    piece_refs, refs = refs[:n_pieces], refs[n_pieces:]
    down, refs = refs[0], refs[1:]
    if not first:
        acc, refs = refs[0], refs[1:]
    if last:
        slope, to_gate, to_up, threshold_ref, width_ref = refs[:5]
        refs = refs[5:]
    local = piece_refs[0].shape[1]
    blocks = [block_of(p, local, chips) for p in spots]

    def work(hid):
        left = jnp.concatenate(whole_pieces(piece_refs, (steps * tokens, local)), axis=1)
        total = nt(left, jnp.concatenate([down[hid, here] for here in blocks], axis=1))
        if not first:
            total = total + acc[:, hid]
        if not last:
            refs[0][:, hid] = total
            return
        threshold, _ = levels(threshold_ref, width_ref, hid)
        parts = step_rows(steps, tokens)
        grads = spikes_back([slope[r, hid] for r in parts], [total[r] for r in parts], threshold)
        grad = jnp.concatenate(grads, axis=0)
        refs[0][:, hid] = (grad * to_gate[:, hid]).astype(bf16)
        refs[1][:, hid] = (grad * to_up[:, hid]).astype(bf16)

    over_tiles(down.shape[0], 512 if last else 1024, work)


def slopes_kernel(steps, tokens, gate, up, threshold_ref, width_ref, slope, to_gate, to_up):
    def work(hid):
        threshold, scale = levels(threshold_ref, width_ref, hid)
        gate_in, up_in = gate[:, hid], up[:, hid]
        sig = sigmoid(gate_in)
        act = gate_in * sig
        hidden = act * up_in
        parts = step_rows(steps, tokens)
        out = spikes_of([hidden[r] for r in parts], threshold, scale)
        slope[:, hid] = jnp.concatenate(slopes_of(out, scale), axis=0)
        to_gate[:, hid] = up_in * (sig * (1.0 + gate_in * (1.0 - sig)))
        to_up[:, hid] = act

    over_tiles(gate.shape[1], 256, work)


def input_grad_kernel(chips, spots, gate_grad, up_grad, gate_w, up_w, *outs):
    left = jnp.concatenate([gate_grad[...], up_grad[...]], axis=1)
    for p, out in zip(spots, outs):
        here = block_of(p, out.shape[1], chips)
        right = jnp.concatenate([gate_w[here, :], up_w[here, :]], axis=1)
        out[...] = nt(left, right).astype(out.dtype)


def per_device(
    devices,
    layer_input,
    gate_weight,
    up_weight,
    down_weight,
    hidden_threshold,
    hidden_width,
    out_threshold,
    out_width,
    out_cotangent,
):
    local = layer_input.shape[1]
    steps = layer_input.shape[2]
    tokens = layer_input.shape[3]
    rows = steps * tokens
    half = rows // 2
    hid = gate_weight.shape[2]
    chips = devices // 2
    far = chips // 2
    side = chips // 2

    order = [2 * p if p < side else 2 * (chips - 1 - p) + 1 for p in range(chips)]
    forward, backward, sibling = [], [], []
    for p in range(chips):
        a, b = order[p], order[(p + 1) % chips]
        for core in range(2):
            forward.append((2 * a + core, 2 * b + core))
            backward.append((2 * b + core, 2 * a + core))
            sibling.append((2 * a + core, 2 * a + 1 - core))
    send_fw = lambda v: lax.ppermute(v, "dp", forward)
    send_bw = lambda v: lax.ppermute(v, "dp", backward)
    swap = lambda v: lax.ppermute(v, "dp", sibling)

    x = turned(layer_input[0])
    cot = turned(out_cotangent[0])

    gate_hbm, up_hbm, down_hbm = gate_weight[0], up_weight[0], down_weight[0]
    spots = lambda at: [(d % chips) * 2 + s for d, s in at]

    def gathered(mine, take, beside, early):
        held, own, sib = None, [], []
        fw = bw = mine

        def taken(new, last=False):
            pieces = [p for v, _ in new for p in (v if isinstance(v, tuple) else (v,))]
            return take(pieces, [at for _, at in new], held, last)

        def swapped(new):
            return [
                (tuple(map(swap, v)) if isinstance(v, tuple) else swap(v), (d, True)) for v, (d, _) in new
            ]

        for k in range(1, far + 1):
            sent = (fw[:half], bw[half:]) if k == far else (fw, bw)
            if early:
                next_fw, next_bw = send_fw(sent[0]), send_bw(sent[1])
            else:
                next_bw, next_fw = send_bw(sent[1]), send_fw(sent[0])
            if k == 1:
                own = [(mine, (0, False))]
                sib = own + swapped(own)
            else:
                own = [(fw, (1 - k, False)), (bw, (k - 1, False))]
                held, sib = taken(own + sib), swapped(own)
                if k == far and early:
                    held, sib = taken(sib), []
            fw, bw = next_fw, next_bw
            bw, held, _ = lax.optimization_barrier((bw, held, beside.get(k)))
            fw = tied(fw, (held, bw) if not early else held)
            if early:
                bw = tied(bw, held)
        own = [((fw, bw), (-far, False))]
        last = swapped(own)
        held = taken(own + sib)
        return taken(last, last=True)

    def scattered(blocks_of, parts):
        def group(k):
            return [(d, s) for s in (False, True) for d in ([k, -k] if k else [0])]

        def sums(own, sib):
            return [o + s.astype(f32) for o, s in zip(own, sib)]

        sib = swap(blocks_of([(far, True)], None)[0])
        first = blocks_of([(far, False)] + group(far - 1)[2:], None)
        total = first[0] + sib.astype(f32)
        fw, bw = total[:half].astype(bf16), total[half:].astype(bf16)
        now_own, now_sib = None, first[1:]
        cut = [slice(p * rows // parts, (p + 1) * rows // parts) for p in range(parts)]
        for k in range(1, far):
            after = fw, bw
            fw, bw = send_fw(fw), send_bw(bw)
            now_sib = [swap(v) for v in now_sib]
            if k == 1:
                now_own = blocks_of(group(far - 1)[:2], after)
                fw, now_own = lax.optimization_barrier((fw, now_own))
            later = blocks_of(group(far - k - 1), after)
            fw, later = lax.optimization_barrier((fw, later))
            bw = tied(bw, later)
            a, b = sums(now_own, now_sib)
            if k == 1:
                fw = jnp.concatenate([a[:half] + fw.astype(f32), a[half:]], axis=0).astype(bf16)
                bw = jnp.concatenate([b[:half], b[half:] + tied(bw, fw).astype(f32)], axis=0).astype(bf16)
            else:
                fw = (a + fw.astype(f32)).astype(bf16)
                bw = (b + tied(bw, fw).astype(f32)).astype(bf16)
            now_own, now_sib = later[: len(later) // 2], later[len(later) // 2 :]
        ends = [(send_fw(fw[c]), send_bw(bw[c])) for c in cut]
        return now_own[0], swap(now_sib[0]), [e[0] for e in ends], [e[1] for e in ends], cut

    hid_level, hid_spread = hidden_threshold, hidden_width
    gate_w, up_w = call(None, [], fetch=(tied(gate_hbm, x), up_hbm))[1]
    down_w = None

    def take_inputs(pieces, at, acc, last):
        nonlocal down_w
        first = acc is None
        args = [*pieces, gate_w, up_w]
        aliases = {}
        if not first:
            aliases = {len(args): 0, len(args) + 1: 1}
            args += list(acc)
        outs = [((rows, hid), f32)] * 2
        if last:
            args += [hid_level, hid_spread]
            outs = outs + [((rows, hid), bf16)]
        res, new = call(
            functools.partial(gate_up_kernel, chips, spots(at), len(pieces), first, last, steps, tokens),
            outs,
            *args,
            flops=0,
            aliases=aliases,
            fetch=(down_hbm,) if first else (),
        )
        if new:
            down_w = new[0]
        return res

    gate, upward, spikes = gathered(x, take_inputs, {1: (gate_w, up_w)}, False)

    def blocks(kernel, flops, *args):
        def blocks_of(at, after):
            outs = [((rows, local), bf16 if s else f32) for _, s in at]
            first = args[0] if after is None else tied(args[0], after)
            return call(functools.partial(kernel, chips, spots(at)), outs, first, *args[1:], flops=len(at) * flops)[0]

        return blocks_of

    own, sib, fw, bw, _ = scattered(blocks(down_kernel, 2 * rows * hid * local, spikes, down_w), 1)
    (emitted, current_grad, grad16), _ = call(
        functools.partial(out_kernel, steps, tokens),
        [((rows, local), bf16), ((rows, local), f32), ((rows, local), bf16)],
        own, sib, fw[0], bw[0], x, cot, out_threshold, out_width,
    )

    sections = lax.axis_size("section")
    incoming = lax.ppermute(emitted, "section", [(s, s + 1) for s in range(sections - 1)])
    way_back, _ = call(
        functools.partial(slopes_kernel, steps, tokens),
        [((rows, hid), f32)] * 3,
        tied(gate, grad16), upward, hid_level, hid_spread,
        flops=2 * rows * hid * local,
    )

    def take_grads(pieces, at, acc, last):
        first = acc is None
        args = [*pieces, down_w]
        aliases = {}
        if not first:
            if not last:
                aliases = {len(args): 0}
            args += acc
        outs = [((rows, hid), f32)]
        if last:
            args += [*way_back, hid_level, hid_spread]
            outs = [((rows, hid), bf16)] * 2
        return call(
            functools.partial(spike_grad_kernel, chips, spots(at), len(pieces), first, last, steps, tokens),
            outs,
            *args,
            flops=2 * rows * hid * local * len(at),
            aliases=aliases,
        )[0]

    gate_grad, up_grad = gathered(grad16, take_grads, {1: way_back}, True)

    own, sib, fw, bw, cut = scattered(
        blocks(input_grad_kernel, 4 * rows * hid * local, gate_grad, up_grad, gate_w, up_w), 1
    )
    returned = []
    for c, from_fw, from_bw in zip(cut, fw, bw):
        total = own[c] + sib[c].astype(f32) + current_grad[c] + from_fw.astype(f32) + from_bw.astype(f32)
        returned.append(
            lax.ppermute(total.astype(bf16), "section", [(s + 1, s) for s in range(sections - 1)])
        )

    def viewed(v):
        return jnp.transpose(v.reshape(steps, tokens, local), (2, 0, 1))[None]

    return viewed(incoming), viewed(jnp.concatenate(returned, axis=0))


def solution(mesh):
    placed = (
        P("section", "dp", None, None),
        P("section", None, "dp"),
        P("section", None, "dp"),
        P("section", "dp", None),
        P("section", "dp"),
        P("section", "dp"),
        P("section", "dp"),
        P("section", "dp"),
        P("section", "dp", None, None),
    )
    return jax.shard_map(
        functools.partial(per_device, mesh.shape["dp"]),
        mesh=mesh,
        in_specs=placed,
        out_specs=(P("section", "dp", None, None), P("section", "dp", None, None)),
        check_vma=False,
    )
```
